32 devices in a mesh: parts: 1, row: 16 (over z, y, core), col: 2 (over x).
Axes of the slice: x: 2, y: 2, z: 4, core: 2. Of those that a mesh axis runs over, the one named last changes fastest.
Arguments:
- pair_act: bfloat16 [256, 256, 128], P(('parts', 'row'), 'col'), may hold values from -6 to 6
- in_weights: bfloat16 [2, 128, 640], replicated, may hold values from -0.5 to 0.5
- out_weights: bfloat16 [2, 128, 128], replicated, may hold values from -0.5 to 0.5
- chain_lengths: int32 [8], P('parts'), may hold values from 1 to 64, 256 in all
Outputs:
- pair_out: bfloat16 [256, 256, 128], P(('parts', 'row'), 'col')
The draws below stay inside these ranges and needn't reach their ends.
Inputs may be any that keep to these rules, and one draw needn't show every extreme that they name: `chain_lengths`: the first 7 entries are chain lengths, the last counts padding residues at the end of the complex; all entries sum to 256, and the largest entry equals 64.
All inputs are finite; a program needn't handle non-finite values.
Results may differ from the reference program's by a relative error of at most 0.0095.
Values may be sent and summed in bfloat16 or wider, within the bound.
No kernel may reach another device: no remote copies, remote signals or barrier semaphores. Data moves between devices by JAX's collectives and lax.ppermute only.
A program may use at most 64 MiB of HBM per device.

```python
import math
import jax
import jax.numpy as jnp
import numpy as np
from jax import lax

C = 128
CHAINS = 8
N = 256


def level_of(rng, shape, cuts, low, top_value):
    level, own = 1.0, jax.random.fold_in(rng, 6)
    for dim, parts in cuts:
        steps = jnp.exp(jax.random.uniform(jax.random.fold_in(own, dim), (parts,), jnp.float32, low / len(cuts), top_value / len(cuts)))
        level = level * jnp.repeat(steps, shape[dim] // parts).reshape([-1 if axis == dim else 1 for axis in range(len(shape))])
    return level


def split_up(amount, total, reach, skew):
    loads = [(1 << 20) // math.isqrt(grade ** skew) + 1 for grade in range(2, amount + 1)]
    surplus, given = total - reach - (amount - 1), [1] * (amount - 1)
    while surplus > 0:
        candidates = [i for i in range(amount - 1) if given[i] < reach]
        whole, budget = sum([loads[i] for i in candidates]), surplus
        for i in candidates:
            extra = min(reach - given[i], max(1, budget * loads[i] // whole), surplus)
            given[i] = given[i] + extra
            surplus = surplus - extra
    return np.array([reach] + given)


def uneven(key, number_of, total, bound, skew):
    if number_of == 2:
        one = jax.random.randint(key, (), max(1, total - bound), min(bound, total - 1) + 1)
        return jnp.stack([one, total - one])
    tallies = jnp.asarray(split_up(number_of, total, bound, skew), jnp.int32)
    couples = (number_of - 1) // 2
    source_of, receiver = tallies[1:1 + 2 * couples:2], tallies[2:2 + 2 * couples:2]
    room = jnp.minimum(source_of - 1, bound - receiver)
    moved = jax.random.randint(jax.random.fold_in(key, 1), (couples,), 0, 1 << 20) % (room + 1)
    tallies = tallies.at[1:1 + 2 * couples:2].set(source_of - moved).at[2:2 + 2 * couples:2].set(receiver + moved)
    return tallies[jax.random.permutation(jax.random.fold_in(key, 2), number_of)]


def normal_values(rng, dims, deviation, limit, pieces=(), held_as=jnp.bfloat16):
    factor_of = level_of(rng, dims, pieces, -0.22, 0.18) if pieces else 1.0
    array = jax.random.normal(rng, dims, jnp.float32) * deviation * factor_of
    return jnp.minimum(jnp.maximum(array, -limit), limit).astype(held_as)


def setup_inputs(seed: int = 0, part: int = 0) -> dict:
    keys = jax.random.split(jax.random.key(seed), 5)
    part_splits = jax.random.split(jax.random.fold_in(keys[4], part), 5)
    pair_act = normal_values(part_splits[0], (N, N, C), 1.0, 6.0, ((0, 16), (1, 2)))
    in_weights = normal_values(keys[1], (2, C, 5 * C), C ** -0.5, 0.5)
    out_weights = normal_values(keys[2], (2, C, C), C ** -0.5, 0.5)
    chain_lengths = uneven(part_splits[3], CHAINS, N, N // 4, 2).astype(jnp.int32)
    return {"pair_act": pair_act, "in_weights": in_weights, "out_weights": out_weights, "chain_lengths": chain_lengths}


epsilon = 1e-05

def layer_norm(values, along_axis):
    mean_vals = lax.optimization_barrier(jnp.mean(values, axis=along_axis, keepdims=True))
    centred = values - mean_vals
    variance = lax.optimization_barrier(jnp.mean(centred * centred, axis=along_axis, keepdims=True))
    return centred * lax.rsqrt(variance + epsilon)

def update(pair_act, weights_in, weights_out, valid, incoming):
    block_rows = math.gcd(N, 64)
    groups = N // block_rows
    blocks = pair_act.reshape(groups, block_rows, N, C)
    valid_blocks = valid.reshape(groups, block_rows)

    def project(inputs):
        block_vals, block_valid = inputs
        normed = layer_norm(block_vals.astype(jnp.float32), 2).astype(jnp.bfloat16)
        projected = jnp.dot(normed.reshape(block_rows * N, C), weights_in, preferred_element_type=jnp.float32).reshape(block_rows, N, 5 * C)
        pair_mask = (block_valid[:, None] * valid[None, :])[:, :, None]
        left_vals = (jax.nn.sigmoid(projected[:, :, 0:C]) * projected[:, :, C:2 * C] * pair_mask).astype(jnp.bfloat16)
        right_vals = (jax.nn.sigmoid(projected[:, :, 2 * C:3 * C]) * projected[:, :, 3 * C:4 * C] * pair_mask).astype(jnp.bfloat16)
        gate_vals = jax.nn.sigmoid(projected[:, :, 4 * C:5 * C]).astype(jnp.bfloat16)
        return (left_vals, right_vals, gate_vals)
    left_vals, right_vals, gate_vals = lax.map(project, (blocks, valid_blocks))
    left_chan = jnp.moveaxis(left_vals.reshape(N, N, C), 2, 0)
    right_chan = jnp.moveaxis(right_vals.reshape(N, N, C), 2, 0)

    def contract(inputs):
        left_one, right_one = inputs
        if incoming:
            product = jnp.dot(left_one.T, right_one, preferred_element_type=jnp.float32)
        else:
            product = jnp.dot(left_one, right_one.T, preferred_element_type=jnp.float32)
        return product.astype(jnp.bfloat16)
    triangle = lax.map(contract, (left_chan, right_chan))
    tri_blocks = jnp.moveaxis(triangle, 0, 2).reshape(groups, block_rows, N, C)

    def finish(inputs):
        block_vals, tri_vals, gate_one = inputs
        tri_normed = layer_norm(tri_vals.astype(jnp.float32), 2).astype(jnp.bfloat16)
        delta_vals = jnp.dot(tri_normed.reshape(block_rows * N, C), weights_out, preferred_element_type=jnp.float32).reshape(block_rows, N, C)
        delta_vals = delta_vals * gate_one.astype(jnp.float32)
        return (block_vals.astype(jnp.float32) + delta_vals).astype(jnp.bfloat16)
    return lax.map(finish, (blocks, tri_blocks, gate_vals)).reshape(N, N, C)

def reference(pair_act, in_weights, out_weights, chain_lengths):
    positions = jnp.arange(N, dtype=jnp.int32)
    valid = (positions < (N - chain_lengths[CHAINS - 1]).astype(jnp.int32)).astype(jnp.float32)
    first_pass = update(pair_act, in_weights[0], out_weights[0], valid, False)
    return update(first_pass, in_weights[1], out_weights[1], valid, True)
```

```python
import functools

import jax
import jax.numpy as jnp
from jax import lax
from jax.experimental import pallas as pl
from jax.experimental.pallas import tpu as pltpu
from jax.sharding import PartitionSpec as P

epsilon = 1e-05
F32 = jnp.float32
BF16 = jnp.bfloat16
VMEM_LIMIT = 32 * 1024 * 1024


def layer_norm(values, along_axis):
    mean_vals = jnp.mean(values, axis=along_axis, keepdims=True)
    centred = values - mean_vals
    variance = jnp.mean(centred * centred, axis=along_axis, keepdims=True)
    return centred * lax.rsqrt(variance + epsilon)


def sigmoid(values):
    return 0.5 * jnp.tanh(0.5 * values) + 0.5


def dot(lhs, rhs):
    return jnp.dot(lhs, rhs, preferred_element_type=F32)


def mask_of(limits_ref, first, group, cols):
    lane = lax.broadcasted_iota(jnp.int32, (1, cols), 1)
    col_valid = lane < limits_ref[1]
    parts = [
        jnp.where(jnp.logical_and(col_valid, first + g < limits_ref[0]), 1.0, 0.0)
        for g in range(group)
    ]
    return jnp.concatenate(parts, axis=1).astype(F32)


def project_rows(first, group, pair_vals, mask, weights_t, left_scr, right_scr, gate_ref):
    width = pair_vals.shape[0]
    cols = pair_vals.shape[1] // group
    normed = layer_norm(pair_vals, 0).astype(BF16)
    for side, scr in enumerate((left_scr, right_scr)):
        both = dot(weights_t[2 * side * width : (2 * side + 2) * width, :], normed)
        vals = sigmoid(both[0:width]) * both[width : 2 * width] * mask
        for g in range(group):
            scr[(first + g) * width : (first + g + 1) * width, :] = vals[
                :, g * cols : (g + 1) * cols
            ]
    gate = sigmoid(dot(weights_t[4 * width : 5 * width, :], normed)).astype(BF16)
    for g in range(group):
        gate_ref[first + g] = gate[:, g * cols : (g + 1) * cols]


def send_channels(rows, width, left_scr, right_scr, send_ref):
    per = send_ref.shape[2]
    for c in range(width):
        for side, scr in enumerate((left_scr, right_scr)):
            send_ref[c // per, side, c % per] = scr[pl.ds(c, rows, stride=width), :].astype(BF16)


def first_kernel(limits_ref, pair_ref, weights_ref, send_ref, gate_ref, pair_t_ref, left_scr, right_scr, wt_scr):
    rows, cols, width = pair_ref.shape
    group = 2
    wt_scr[...] = weights_ref[0].astype(F32).T.astype(BF16)
    for first in range(0, rows, group):
        blocks = [pair_ref[first + g].astype(F32).T for g in range(group)]
        for g in range(group):
            pair_t_ref[first + g] = blocks[g].astype(BF16)
        project_rows(
            first, group, jnp.concatenate(blocks, axis=1), mask_of(limits_ref, first, group, cols),
            wt_scr, left_scr, right_scr, gate_ref,
        )
    send_channels(rows, width, left_scr, right_scr, send_ref)


def finish_rows(first, group, tri_scr, rows, wo_t, gate_ref, pair_t_ref):
    width = pair_t_ref.shape[1]
    tri = jnp.concatenate(
        [tri_scr[pl.ds(first + g, width, stride=rows), :] for g in range(group)], axis=1
    )
    tri_normed = layer_norm(tri, 0).astype(BF16)
    delta = dot(wo_t, tri_normed)
    gate = jnp.concatenate([gate_ref[first + g] for g in range(group)], axis=1)
    pair = jnp.concatenate([pair_t_ref[first + g] for g in range(group)], axis=1)
    return (pair.astype(F32) + delta * gate.astype(F32)).astype(BF16)


def middle_kernel(
    limits_ref, tri_ref, gate_in_ref, pair_t_in_ref, wo_ref, weights_ref,
    send_ref, gate_ref, pair_t_ref, left_scr, right_scr, wt_scr, tri_scr,
):
    width, rows, cols = tri_ref.shape
    group = 2
    wt_scr[...] = weights_ref[1].astype(F32).T.astype(BF16)
    wo_t = wo_ref[0].astype(F32).T.astype(BF16)
    tri_scr[...] = tri_ref[...].astype(F32).reshape(width * rows, cols)
    for first in range(0, rows, group):
        passed = finish_rows(first, group, tri_scr, rows, wo_t, gate_in_ref, pair_t_in_ref)
        for g in range(group):
            pair_t_ref[first + g] = passed[:, g * cols : (g + 1) * cols]
        project_rows(
            first, group, passed.astype(F32), mask_of(limits_ref, first, group, cols),
            wt_scr, left_scr, right_scr, gate_ref,
        )
    send_channels(rows, width, left_scr, right_scr, send_ref)


def last_kernel(tri_ref, gate_ref, pair_t_ref, wo_ref, out_ref, tri_scr):
    width, rows, cols = tri_ref.shape
    group = 2
    wo_t = wo_ref[1].astype(F32).T.astype(BF16)
    tri_scr[...] = tri_ref[...].astype(F32).reshape(width * rows, cols)
    for first in range(0, rows, group):
        passed = finish_rows(first, group, tri_scr, rows, wo_t, gate_ref, pair_t_ref)
        for g in range(group):
            out_ref[first + g] = passed[:, g * cols : (g + 1) * cols].astype(F32).T.astype(BF16)


def triangle_kernel(incoming, recv_ref, out_ref):
    n_row, n_col, _, per, rows, cols = recv_ref.shape
    for c in range(per):
        left, right = (
            jnp.concatenate(
                [recv_ref[:, x, side, c].reshape(n_row * rows, cols) for x in range(n_col)], axis=1
            )
            for side in (0, 1)
        )
        dims = (((0,), (0,)), ((), ())) if incoming else (((1,), (1,)), ((), ()))
        tri = lax.dot_general(left, right, dims, preferred_element_type=F32).astype(BF16)
        for x in range(n_col):
            out_ref[:, x, c] = tri[:, x * cols : (x + 1) * cols].reshape(n_row, rows, cols)


def call(kernel, name, out_shape, scratch, in_specs, flops, *args):
    return pl.pallas_call(
        kernel,
        name=name,
        out_shape=out_shape,
        in_specs=in_specs,
        out_specs=jax.tree.map(lambda _: pl.BlockSpec(memory_space=pltpu.VMEM), out_shape),
        scratch_shapes=scratch,
        compiler_params=pltpu.CompilerParams(vmem_limit_bytes=VMEM_LIMIT),
        cost_estimate=pl.CostEstimate(flops=flops, bytes_accessed=2 << 20, transcendentals=0),
    )(*args)


VM = pl.BlockSpec(memory_space=pltpu.VMEM)
SM = pl.BlockSpec(memory_space=pltpu.SMEM)


def split_channels(n_row, n_col, pair_act, in_weights, out_weights, chain_lengths):
    rows, cols, width = pair_act.shape
    group = n_row * n_col
    per = width // group
    axes = ("row", "col")
    count_valid = rows * n_row - chain_lengths[chain_lengths.shape[0] - 1]
    limits = jnp.stack(
        [count_valid - lax.axis_index("row") * rows, count_valid - lax.axis_index("col") * cols]
    ).astype(jnp.int32)

    send_shape = jax.ShapeDtypeStruct((group, 2, per, rows, cols), BF16)
    block_shape = jax.ShapeDtypeStruct((rows, width, cols), BF16)
    tri_shape = jax.ShapeDtypeStruct((n_row, n_col, per, rows, cols), BF16)
    scr = pltpu.VMEM((rows * width, cols), F32)
    wt_scr = pltpu.VMEM((5 * width, width), BF16)
    flops_in = 2 * rows * cols * width * 5 * width
    flops_out = 2 * rows * cols * width * width
    flops_tri = 2 * per * (n_row * rows) ** 2 * n_col * cols

    def exchange(array):
        return lax.all_to_all(array, axes, split_axis=0, concat_axis=0, tiled=True)

    def triangle(send, incoming):
        recv = exchange(send).reshape((n_row, n_col) + send.shape[1:])
        tri = call(
            functools.partial(triangle_kernel, incoming), "triangle", tri_shape, [], [VM], flops_tri, recv
        )
        return exchange(tri.reshape((group,) + tri.shape[2:])).reshape(width, rows, cols)

    send, gate, pair_t = call(
        first_kernel, "project", (send_shape, block_shape, block_shape), [scr, scr, wt_scr],
        [SM, VM, VM], flops_in, limits, pair_act, in_weights,
    )
    tri = triangle(send, False)
    send, gate, pair_t = call(
        middle_kernel, "finish_project", (send_shape, block_shape, block_shape), [scr, scr, wt_scr, scr],
        [SM, VM, VM, VM, VM, VM], flops_in + flops_out,
        limits, tri, gate, pair_t, out_weights, in_weights,
    )
    tri = triangle(send, True)
    return call(
        last_kernel, "finish", jax.ShapeDtypeStruct(pair_act.shape, BF16), [scr],
        [VM, VM, VM, VM], flops_out, tri, gate, pair_t, out_weights,
    )


def project(pair_act, weights, pair_mask):
    width = pair_act.shape[2]
    normed = layer_norm(pair_act.astype(F32), 2).astype(BF16)
    projected = jnp.einsum("rjd,de->erj", normed, weights[:, 0 : 4 * width], preferred_element_type=F32)
    left_vals = (jax.nn.sigmoid(projected[0:width]) * projected[width : 2 * width] * pair_mask).astype(BF16)
    right_vals = (
        jax.nn.sigmoid(projected[2 * width : 3 * width]) * projected[3 * width : 4 * width] * pair_mask
    ).astype(BF16)
    gate_vals = jax.nn.sigmoid(
        jnp.einsum("rjd,de->rje", normed, weights[:, 4 * width : 5 * width], preferred_element_type=F32)
    ).astype(BF16)
    return (left_vals, right_vals, gate_vals)


def to_channels(left_vals, right_vals):
    return (
        lax.all_to_all(left_vals, "row", split_axis=0, concat_axis=1, tiled=True),
        lax.all_to_all(right_vals, "row", split_axis=0, concat_axis=1, tiled=True),
    )


def finish(pair_act, triangle, gate_vals, weights_out):
    tri_normed = layer_norm(triangle.astype(F32), 0).astype(BF16)
    delta_vals = jnp.einsum("crj,cd->rjd", tri_normed, weights_out, preferred_element_type=F32)
    delta_vals = delta_vals * gate_vals.astype(F32)
    return (pair_act.astype(F32) + delta_vals).astype(BF16)


def split_rows(pair_act, in_weights, out_weights, chain_lengths):
    row_tile = pair_act.shape[0]
    col_tile = pair_act.shape[1]
    total_rows = row_tile * lax.axis_size("row")
    count_valid = total_rows - chain_lengths[chain_lengths.shape[0] - 1]
    row_first = lax.axis_index("row") * row_tile
    col_first = lax.axis_index("col") * col_tile
    row_valid = (row_first + jnp.arange(row_tile, dtype=jnp.int32) < count_valid).astype(F32)
    col_valid = (col_first + jnp.arange(col_tile, dtype=jnp.int32) < count_valid).astype(F32)
    pair_mask = row_valid[:, None] * col_valid[None, :]
    left_vals, right_vals, gate_vals = project(pair_act, in_weights[0], pair_mask)
    left_chan, right_chan = to_channels(left_vals, right_vals)
    left_rows = lax.all_to_all(left_chan, "col", split_axis=1, concat_axis=2, tiled=True)
    summed = jnp.einsum(
        "cik,cjk->cij",
        left_rows,
        lax.all_gather(right_chan, "col", axis=2, tiled=True),
        preferred_element_type=F32,
    )
    triangle = lax.all_to_all(
        lax.all_to_all(summed.astype(BF16), "col", split_axis=2, concat_axis=1, tiled=True),
        "row",
        split_axis=1,
        concat_axis=0,
        tiled=True,
    )
    first_pass = finish(pair_act, triangle, gate_vals, out_weights[0])
    left_vals, right_vals, gate_vals = project(first_pass, in_weights[1], pair_mask)
    left_chan, right_chan = to_channels(left_vals, right_vals)
    summed_in = jnp.einsum(
        "cki,ckj->cij",
        lax.all_gather(left_chan, "col", axis=2, tiled=True),
        right_chan,
        preferred_element_type=F32,
    ).astype(BF16)
    triangle_in = lax.all_to_all(summed_in, "row", split_axis=1, concat_axis=0, tiled=True)
    return finish(first_pass, triangle_in, gate_vals, out_weights[1])


def solution(mesh):
    n_row, n_col = mesh.shape["row"], mesh.shape["col"]

    def per_device(pair_act, in_weights, out_weights, chain_lengths):
        if pair_act.shape[2] % (n_row * n_col) == 0:
            return split_channels(n_row, n_col, pair_act, in_weights, out_weights, chain_lengths)
        return split_rows(pair_act, in_weights, out_weights, chain_lengths)

    in_specs = (P(("parts", "row"), "col", None), P(), P(), P("parts"))
    out_specs = P(("parts", "row"), "col", None)
    return jax.shard_map(
        per_device, mesh=mesh, in_specs=in_specs, out_specs=out_specs, check_vma=False
    )
```

```python
import functools

import jax
import jax.numpy as jnp
from jax import lax
from jax.experimental import pallas as pl
from jax.experimental.pallas import tpu as pltpu
from jax.sharding import PartitionSpec as P

epsilon = 1e-05
F32 = jnp.float32
BF16 = jnp.bfloat16
VMEM_LIMIT = 32 * 1024 * 1024


def layer_norm(values, along_axis):
    mean_vals = jnp.mean(values, axis=along_axis, keepdims=True)
    centred = values - mean_vals
    variance = jnp.mean(centred * centred, axis=along_axis, keepdims=True)
    return centred * lax.rsqrt(variance + epsilon)


def sigmoid(values):
    return 0.5 * jnp.tanh(0.5 * values) + 0.5


def dot(lhs, rhs):
    return jnp.dot(lhs, rhs, preferred_element_type=F32)


def mask_of(limits, first, group, cols):
    lane = lax.broadcasted_iota(jnp.int32, (1, cols), 1)
    col_valid = lane < limits[1]
    parts = [
        jnp.where(jnp.logical_and(col_valid, first + g < limits[0]), 1.0, 0.0) for g in range(group)
    ]
    return jnp.concatenate(parts, axis=1).astype(F32)


def limits_of(lengths_ref, rows, cols):
    valid = rows * lax.axis_size("row") - lengths_ref[lengths_ref.shape[0] - 1]
    return valid - lax.axis_index("row") * rows, valid - lax.axis_index("col") * cols


def store_rows(ref, first, group, vals):
    cols = vals.shape[1] // group
    for g in range(group):
        ref[first + g] = vals[:, g * cols : (g + 1) * cols]


def load_rows(ref, first, group):
    return jnp.concatenate([ref[first + g] for g in range(group)], axis=1)


def project_rows(first, group, pair_vals, mask, weights_t, left_scr, right_scr, gate_ref):
    width = pair_vals.shape[0]
    normed = layer_norm(pair_vals, 0).astype(BF16)
    for side, scr in enumerate((left_scr, right_scr)):
        both = dot(weights_t[2 * side * width : (2 * side + 2) * width, :], normed)
        vals = sigmoid(both[0:width]) * both[width : 2 * width] * mask
        store_rows(scr, first, group, vals.astype(BF16))
    gate = sigmoid(dot(weights_t[4 * width : 5 * width, :], normed))
    store_rows(gate_ref, first, group, gate.astype(BF16))


def send_channels(left_scr, right_scr, send_ref):
    rows, width, cols = left_scr.shape
    group, _, per = send_ref.shape[:3]
    for side, scr in enumerate((left_scr, right_scr)):
        send_ref[:, side] = jnp.swapaxes(scr[...], 0, 1).reshape(group, per, rows, cols)


def first_kernel(
    lengths_ref, pair_hbm, weights_hbm, send_ref, gate_ref, pair_t_ref,
    left_scr, right_scr, wt_scr, pair_scr, weights_scr, sems,
):
    rows, cols, width = pair_scr.shape
    group = 2
    copies = [
        pltpu.make_async_copy(weights_hbm.at[0], weights_scr, sems.at[0]),
        pltpu.make_async_copy(pair_hbm, pair_scr, sems.at[1]),
    ]
    for copy in copies:
        copy.start()
    limits = limits_of(lengths_ref, rows, cols)
    copies[0].wait()
    wt_scr[...] = weights_scr[...].T
    copies[1].wait()
    for first in range(0, rows, group):
        blocks = jnp.concatenate([pair_scr[first + g].T for g in range(group)], axis=1)
        store_rows(pair_t_ref, first, group, blocks)
        project_rows(
            first, group, blocks.astype(F32), mask_of(limits, first, group, cols),
            wt_scr, left_scr, right_scr, gate_ref,
        )
    send_channels(left_scr, right_scr, send_ref)


def finish_rows(first, group, tri_scr, wo_t, gate_ref, pair_t_ref):
    tri = load_rows(tri_scr, first, group).astype(F32)
    delta = dot(wo_t, layer_norm(tri, 0).astype(BF16))
    gate = load_rows(gate_ref, first, group).astype(F32)
    return (load_rows(pair_t_ref, first, group).astype(F32) + delta * gate).astype(BF16)


def middle_kernel(
    lengths_ref, tri_ref, gate_in_ref, pair_t_in_ref, wo_ref, weights_ref,
    send_ref, gate_ref, pair_t_ref, left_scr, right_scr, wt_scr, tri_scr,
):
    width, rows, cols = tri_ref.shape
    group = 2
    limits = limits_of(lengths_ref, rows, cols)
    wt_scr[...] = weights_ref[1].T
    wo_t = wo_ref[0].T
    tri_scr[...] = jnp.swapaxes(tri_ref[...], 0, 1)
    for first in range(0, rows, group):
        passed = finish_rows(first, group, tri_scr, wo_t, gate_in_ref, pair_t_in_ref)
        store_rows(pair_t_ref, first, group, passed)
        project_rows(
            first, group, passed.astype(F32), mask_of(limits, first, group, cols),
            wt_scr, left_scr, right_scr, gate_ref,
        )
    send_channels(left_scr, right_scr, send_ref)


def last_kernel(tri_ref, gate_ref, pair_t_ref, wo_ref, out_ref, tri_scr):
    width, rows, cols = tri_ref.shape
    group = 2
    wo_t = wo_ref[1].T
    tri_scr[...] = jnp.swapaxes(tri_ref[...], 0, 1)
    for first in range(0, rows, group):
        passed = finish_rows(first, group, tri_scr, wo_t, gate_ref, pair_t_ref)
        for g in range(group):
            out_ref[first + g] = passed[:, g * cols : (g + 1) * cols].T


def triangle_kernel(incoming, recv_ref, out_ref):
    n_row, n_col, _, per, rows, cols = recv_ref.shape
    for c in range(per):
        left, right = (
            jnp.concatenate(
                [recv_ref[:, x, side, c].reshape(n_row * rows, cols) for x in range(n_col)], axis=1
            )
            for side in (0, 1)
        )
        dims = (((0,), (0,)), ((), ())) if incoming else (((1,), (1,)), ((), ()))
        tri = lax.dot_general(left, right, dims, preferred_element_type=F32).astype(BF16)
        for x in range(n_col):
            out_ref[:, x, c] = tri[:, x * cols : (x + 1) * cols].reshape(n_row, rows, cols)


def call(kernel, name, out_shape, scratch, in_specs, flops, *args):
    return pl.pallas_call(
        kernel,
        name=name,
        out_shape=out_shape,
        in_specs=in_specs,
        out_specs=jax.tree.map(lambda _: pl.BlockSpec(memory_space=pltpu.VMEM), out_shape),
        scratch_shapes=scratch,
        compiler_params=pltpu.CompilerParams(vmem_limit_bytes=VMEM_LIMIT),
        cost_estimate=pl.CostEstimate(flops=flops, bytes_accessed=2 << 20, transcendentals=0),
    )(*args)


VM = pl.BlockSpec(memory_space=pltpu.VMEM)
SM = pl.BlockSpec(memory_space=pltpu.SMEM)
HBM = pl.BlockSpec(memory_space=pltpu.HBM)


def split_channels(n_row, n_col, pair_act, in_weights, out_weights, chain_lengths):
    rows, cols, width = pair_act.shape
    group = n_row * n_col
    per = width // group
    axes = ("row", "col")
    send_shape = jax.ShapeDtypeStruct((group, 2, per, rows, cols), BF16)
    block_shape = jax.ShapeDtypeStruct((rows, width, cols), BF16)
    tri_shape = jax.ShapeDtypeStruct((n_row, n_col, per, rows, cols), BF16)
    scr = pltpu.VMEM((rows, width, cols), BF16)
    wt_scr = pltpu.VMEM((5 * width, width), BF16)
    flops_in = 2 * rows * cols * width * 5 * width
    flops_out = 2 * rows * cols * width * width
    flops_tri = 2 * per * (n_row * rows) ** 2 * n_col * cols

    def exchange(array):
        return lax.all_to_all(array, axes, split_axis=0, concat_axis=0, tiled=True)

    def triangle(send, incoming):
        recv = exchange(send).reshape((n_row, n_col) + send.shape[1:])
        tri = call(
            functools.partial(triangle_kernel, incoming), "triangle", tri_shape, [], [VM], flops_tri, recv
        )
        return exchange(tri.reshape((group,) + tri.shape[2:])).reshape(width, rows, cols)

    send, gate, pair_t = call(
        first_kernel, "project", (send_shape, block_shape, block_shape),
        [
            scr, scr, wt_scr, pltpu.VMEM(pair_act.shape, BF16),
            pltpu.VMEM(in_weights.shape[1:], BF16), pltpu.SemaphoreType.DMA((2,)),
        ],
        [SM, HBM, HBM], flops_in, chain_lengths, pair_act, in_weights,
    )
    tri = triangle(send, False)
    send, gate, pair_t = call(
        middle_kernel, "finish_project", (send_shape, block_shape, block_shape), [scr, scr, wt_scr, scr],
        [SM, VM, VM, VM, VM, VM], flops_in + flops_out,
        chain_lengths, tri, gate, pair_t, out_weights, in_weights,
    )
    tri = triangle(send, True)
    return call(
        last_kernel, "finish", jax.ShapeDtypeStruct(pair_act.shape, BF16), [scr],
        [VM, VM, VM, VM], flops_out, tri, gate, pair_t, out_weights,
    )


def project(pair_act, weights, pair_mask):
    width = pair_act.shape[2]
    normed = layer_norm(pair_act.astype(F32), 2).astype(BF16)
    projected = jnp.einsum("rjd,de->erj", normed, weights[:, 0 : 4 * width], preferred_element_type=F32)
    left_vals = (jax.nn.sigmoid(projected[0:width]) * projected[width : 2 * width] * pair_mask).astype(BF16)
    right_vals = (
        jax.nn.sigmoid(projected[2 * width : 3 * width]) * projected[3 * width : 4 * width] * pair_mask
    ).astype(BF16)
    gate_vals = jax.nn.sigmoid(
        jnp.einsum("rjd,de->rje", normed, weights[:, 4 * width : 5 * width], preferred_element_type=F32)
    ).astype(BF16)
    return (left_vals, right_vals, gate_vals)


def to_channels(left_vals, right_vals):
    return (
        lax.all_to_all(left_vals, "row", split_axis=0, concat_axis=1, tiled=True),
        lax.all_to_all(right_vals, "row", split_axis=0, concat_axis=1, tiled=True),
    )


def finish(pair_act, triangle, gate_vals, weights_out):
    tri_normed = layer_norm(triangle.astype(F32), 0).astype(BF16)
    delta_vals = jnp.einsum("crj,cd->rjd", tri_normed, weights_out, preferred_element_type=F32)
    delta_vals = delta_vals * gate_vals.astype(F32)
    return (pair_act.astype(F32) + delta_vals).astype(BF16)


def split_rows(pair_act, in_weights, out_weights, chain_lengths):
    row_tile = pair_act.shape[0]
    col_tile = pair_act.shape[1]
    total_rows = row_tile * lax.axis_size("row")
    count_valid = total_rows - chain_lengths[chain_lengths.shape[0] - 1]
    row_first = lax.axis_index("row") * row_tile
    col_first = lax.axis_index("col") * col_tile
    row_valid = (row_first + jnp.arange(row_tile, dtype=jnp.int32) < count_valid).astype(F32)
    col_valid = (col_first + jnp.arange(col_tile, dtype=jnp.int32) < count_valid).astype(F32)
    pair_mask = row_valid[:, None] * col_valid[None, :]
    left_vals, right_vals, gate_vals = project(pair_act, in_weights[0], pair_mask)
    left_chan, right_chan = to_channels(left_vals, right_vals)
    left_rows = lax.all_to_all(left_chan, "col", split_axis=1, concat_axis=2, tiled=True)
    summed = jnp.einsum(
        "cik,cjk->cij",
        left_rows,
        lax.all_gather(right_chan, "col", axis=2, tiled=True),
        preferred_element_type=F32,
    )
    triangle = lax.all_to_all(
        lax.all_to_all(summed.astype(BF16), "col", split_axis=2, concat_axis=1, tiled=True),
        "row",
        split_axis=1,
        concat_axis=0,
        tiled=True,
    )
    first_pass = finish(pair_act, triangle, gate_vals, out_weights[0])
    left_vals, right_vals, gate_vals = project(first_pass, in_weights[1], pair_mask)
    left_chan, right_chan = to_channels(left_vals, right_vals)
    summed_in = jnp.einsum(
        "cki,ckj->cij",
        lax.all_gather(left_chan, "col", axis=2, tiled=True),
        right_chan,
        preferred_element_type=F32,
    ).astype(BF16)
    triangle_in = lax.all_to_all(summed_in, "row", split_axis=1, concat_axis=0, tiled=True)
    return finish(first_pass, triangle_in, gate_vals, out_weights[1])


def solution(mesh):
    n_row, n_col = mesh.shape["row"], mesh.shape["col"]

    def per_device(pair_act, in_weights, out_weights, chain_lengths):
        if pair_act.shape[2] % (n_row * n_col) == 0:
            return split_channels(n_row, n_col, pair_act, in_weights, out_weights, chain_lengths)
        return split_rows(pair_act, in_weights, out_weights, chain_lengths)

    in_specs = (P(("parts", "row"), "col", None), P(), P(), P("parts"))
    out_specs = P(("parts", "row"), "col", None)
    return jax.shard_map(
        per_device, mesh=mesh, in_specs=in_specs, out_specs=out_specs, check_vma=False
    )
```

```python
import functools

import jax
import jax.numpy as jnp
from jax import lax
from jax.experimental import pallas as pl
from jax.experimental.pallas import tpu as pltpu
from jax.sharding import PartitionSpec as P

epsilon = 1e-05
F32 = jnp.float32
BF16 = jnp.bfloat16
VMEM_LIMIT = 32 * 1024 * 1024


def layer_norm(values, along_axis):
    mean_vals = jnp.mean(values, axis=along_axis, keepdims=True)
    centred = values - mean_vals
    variance = jnp.mean(centred * centred, axis=along_axis, keepdims=True)
    return centred * lax.rsqrt(variance + epsilon)


def sigmoid(values):
    return 0.5 * jnp.tanh(0.5 * values) + 0.5


def dot(lhs, rhs):
    return jnp.dot(lhs, rhs, preferred_element_type=F32)


def store_mask(ref, row_limit, col_limit):
    row = lax.broadcasted_iota(jnp.int32, ref.shape, 0)
    col = lax.broadcasted_iota(jnp.int32, ref.shape, 1)
    ref[...] = jnp.where(jnp.logical_and(row < row_limit, col < col_limit), 1.0, 0.0).astype(F32)


def load_mask(ref, first, group):
    return jnp.concatenate([ref[first + g : first + g + 1, :] for g in range(group)], axis=1)


def store_rows(ref, first, group, vals):
    cols = vals.shape[1] // group
    for g in range(group):
        ref[first + g] = vals[:, g * cols : (g + 1) * cols]


def load_rows(ref, first, group):
    return jnp.concatenate([ref[first + g] for g in range(group)], axis=1)


def project_side(normed, mask, weights_t, side):
    width = normed.shape[0]
    both = dot(weights_t[2 * side * width : (2 * side + 2) * width, :], normed)
    return (sigmoid(both[0:width]) * both[width : 2 * width] * mask).astype(BF16)


def project_rows(first, group, pair_vals, mask, weights_t, left_scr, right_scr, gate_ref):
    width = pair_vals.shape[0]
    normed = layer_norm(pair_vals, 0).astype(BF16)
    for side, scr in enumerate((left_scr, right_scr)):
        store_rows(scr, first, group, project_side(normed, mask, weights_t, side))
    gate = sigmoid(dot(weights_t[4 * width : 5 * width, :], normed))
    store_rows(gate_ref, first, group, gate.astype(BF16))


def send_channels(scr, send_ref, side):
    rows, width, cols = scr.shape
    group, _, per = send_ref.shape[:3]
    send_ref[:, side] = jnp.swapaxes(scr[...], 0, 1).reshape(group, per, rows, cols)


def first_kernel(
    lengths_ref, pair_ref, weights_ref, send_ref, gate_ref, pair_t_ref, mask_ref, other_mask_ref,
    left_scr, right_scr, wt_scr,
):
    rows, cols, width = pair_ref.shape
    group = 2
    halves, in_half = lax.axis_size("half"), lax.axis_size("row")
    half, row = lax.axis_index("half"), lax.axis_index("row")
    valid = rows * halves * in_half - lengths_ref[lengths_ref.shape[0] - 1]
    col_limit = valid - lax.axis_index("col") * cols
    store_mask(mask_ref, valid - (half * in_half + row) * rows, col_limit)
    store_mask(other_mask_ref, valid - ((1 - half) * in_half + row) * rows, col_limit)
    wt_scr[...] = weights_ref[0].T
    for first in range(0, rows, group):
        blocks = jnp.concatenate([pair_ref[first + g].T for g in range(group)], axis=1)
        store_rows(pair_t_ref, first, group, blocks)
        project_rows(
            first, group, blocks.astype(F32), load_mask(mask_ref, first, group),
            wt_scr, left_scr, right_scr, gate_ref,
        )
    send_channels(left_scr, send_ref, 0)
    send_channels(right_scr, send_ref, 1)


def right_kernel(pair_ref, weights_ref, mask_ref, send_ref, right_scr, wt_scr):
    rows, cols, width = pair_ref.shape
    group = 2
    wt_scr[2 * width : 4 * width, :] = weights_ref[0, :, 2 * width : 4 * width].T
    for first in range(0, rows, group):
        blocks = jnp.concatenate([pair_ref[first + g].T for g in range(group)], axis=1)
        normed = layer_norm(blocks.astype(F32), 0).astype(BF16)
        vals = project_side(normed, load_mask(mask_ref, first, group), wt_scr, 1)
        store_rows(right_scr, first, group, vals)
    send_channels(right_scr, send_ref, 0)


def finish_rows(first, group, tri_scr, wo_t, gate_ref, pair_t_ref):
    tri = load_rows(tri_scr, first, group).astype(F32)
    delta = dot(wo_t, layer_norm(tri, 0).astype(BF16))
    gate = load_rows(gate_ref, first, group).astype(F32)
    return (load_rows(pair_t_ref, first, group).astype(F32) + delta * gate).astype(BF16)


def middle_kernel(
    tri_ref, gate_in_ref, pair_t_in_ref, mask_ref, wo_ref, weights_ref,
    send_ref, gate_ref, pair_t_ref, left_scr, right_scr, wt_scr, tri_scr,
):
    width, rows, cols = tri_ref.shape
    group = 2
    wt_scr[...] = weights_ref[1].T
    wo_t = wo_ref[0].T
    tri_scr[...] = jnp.swapaxes(tri_ref[...], 0, 1)
    for first in range(0, rows, group):
        passed = finish_rows(first, group, tri_scr, wo_t, gate_in_ref, pair_t_in_ref)
        store_rows(pair_t_ref, first, group, passed)
        project_rows(
            first, group, passed.astype(F32), load_mask(mask_ref, first, group),
            wt_scr, left_scr, right_scr, gate_ref,
        )
    send_channels(left_scr, send_ref, 0)
    send_channels(right_scr, send_ref, 1)


def last_kernel(tri_ref, gate_ref, pair_t_ref, wo_ref, out_ref, tri_scr):
    width, rows, cols = tri_ref.shape
    group = 2
    wo_t = wo_ref[1].T
    tri_scr[...] = jnp.swapaxes(tri_ref[...], 0, 1)
    for first in range(0, rows, group):
        passed = finish_rows(first, group, tri_scr, wo_t, gate_ref, pair_t_ref)
        for g in range(group):
            out_ref[first + g] = passed[:, g * cols : (g + 1) * cols].T


def channel_of(recv_ref, side, c):
    n_row, n_col, _, _, rows, cols = recv_ref.shape
    return jnp.concatenate(
        [recv_ref[:, x, side, c].reshape(n_row * rows, cols) for x in range(n_col)], axis=1
    )


def store_channel(out_ref, c, tri):
    n_row, n_col, _, rows, cols = out_ref.shape
    for x in range(n_col):
        out_ref[:, x, c] = tri[:, x * cols : (x + 1) * cols].reshape(n_row, rows, cols)


def outgoing_kernel(own_ref, other_ref, out_ref):
    lower = lax.axis_index("half") == 0
    for c in range(own_ref.shape[3]):
        own, other = channel_of(own_ref, 1, c), channel_of(other_ref, 0, c)
        right = jnp.concatenate(
            [jnp.where(lower, own, other), jnp.where(lower, other, own)], axis=0
        )
        tri = lax.dot_general(
            channel_of(own_ref, 0, c), right, (((1,), (1,)), ((), ())), preferred_element_type=F32
        )
        store_channel(out_ref, c, tri.astype(BF16))


def incoming_kernel(recv_ref, out_ref):
    for c in range(recv_ref.shape[3]):
        tri = lax.dot_general(
            channel_of(recv_ref, 0, c), channel_of(recv_ref, 1, c), (((0,), (0,)), ((), ())),
            preferred_element_type=F32,
        )
        store_channel(out_ref, c, tri.astype(BF16))


def call(kernel, name, out_shape, scratch, in_specs, flops, *args):
    return pl.pallas_call(
        kernel,
        name=name,
        out_shape=out_shape,
        in_specs=in_specs,
        out_specs=jax.tree.map(lambda _: pl.BlockSpec(memory_space=pltpu.VMEM), out_shape),
        scratch_shapes=scratch,
        compiler_params=pltpu.CompilerParams(vmem_limit_bytes=VMEM_LIMIT),
        cost_estimate=pl.CostEstimate(flops=flops, bytes_accessed=2 << 20, transcendentals=0),
    )(*args)


VM = pl.BlockSpec(memory_space=pltpu.VMEM)
SM = pl.BlockSpec(memory_space=pltpu.SMEM)


def split_channels(n_half, n_row, n_col, pair_act, in_weights, out_weights, chain_lengths):
    rows, cols, width = pair_act.shape
    in_half, in_all = ("row", "col"), ("half", "row", "col")
    half_group, group = n_row * n_col, n_half * n_row * n_col
    half_per, per = width // half_group, width // group

    def shape_of(*dims, dtype=BF16):
        return jax.ShapeDtypeStruct(dims, dtype)

    def exchange(array, axes):
        return lax.all_to_all(array, axes, split_axis=0, concat_axis=0, tiled=True)

    block_shape = shape_of(rows, width, cols)
    mask_shape = shape_of(rows, cols, dtype=F32)
    scr = pltpu.VMEM((rows, width, cols), BF16)
    wt_scr = pltpu.VMEM((5 * width, width), BF16)
    flops_out = 2 * rows * cols * width * width
    flops_tri = 2 * per * (n_half * n_row * rows) ** 2 * n_col * cols

    other = lax.ppermute(pair_act, "half", [(0, 1), (1, 0)])
    send, gate, pair_t, mask, other_mask = call(
        first_kernel, "project",
        (shape_of(half_group, 2, half_per, rows, cols), block_shape, block_shape, mask_shape, mask_shape),
        [scr, scr, wt_scr], [SM, VM, VM], 5 * flops_out, chain_lengths, pair_act, in_weights,
    )
    own = exchange(send, in_half).reshape(n_row, n_col, 2, half_per, rows, cols)
    send = call(
        right_kernel, "project_right", shape_of(half_group, 1, half_per, rows, cols),
        [scr, wt_scr], [VM, VM, VM], 2 * flops_out, other, in_weights, other_mask,
    )
    other = exchange(send, in_half).reshape(n_row, n_col, 1, half_per, rows, cols)
    tri = call(
        outgoing_kernel, "outgoing", shape_of(n_row, n_col, half_per, rows, cols),
        [], [VM, VM], flops_tri, own, other,
    )
    tri = exchange(tri.reshape(half_group, half_per, rows, cols), in_half).reshape(width, rows, cols)
    send, gate, pair_t = call(
        middle_kernel, "finish_project", (shape_of(group, 2, per, rows, cols), block_shape, block_shape),
        [scr, scr, wt_scr, scr], [VM] * 6, 6 * flops_out,
        tri, gate, pair_t, mask, out_weights, in_weights,
    )
    recv = exchange(send, in_all).reshape(n_half * n_row, n_col, 2, per, rows, cols)
    tri = call(
        incoming_kernel, "incoming", shape_of(n_half * n_row, n_col, per, rows, cols), [], [VM], flops_tri, recv
    )
    tri = exchange(tri.reshape(group, per, rows, cols), in_all).reshape(width, rows, cols)
    return call(
        last_kernel, "finish", shape_of(*pair_act.shape), [scr], [VM] * 4, flops_out,
        tri, gate, pair_t, out_weights,
    )


def project(pair_act, weights, pair_mask):
    width = pair_act.shape[2]
    normed = layer_norm(pair_act.astype(F32), 2).astype(BF16)
    projected = jnp.einsum("rjd,de->erj", normed, weights[:, 0 : 4 * width], preferred_element_type=F32)
    left_vals = (jax.nn.sigmoid(projected[0:width]) * projected[width : 2 * width] * pair_mask).astype(BF16)
    right_vals = (
        jax.nn.sigmoid(projected[2 * width : 3 * width]) * projected[3 * width : 4 * width] * pair_mask
    ).astype(BF16)
    gate_vals = jax.nn.sigmoid(
        jnp.einsum("rjd,de->rje", normed, weights[:, 4 * width : 5 * width], preferred_element_type=F32)
    ).astype(BF16)
    return (left_vals, right_vals, gate_vals)


def to_channels(left_vals, right_vals):
    return (
        lax.all_to_all(left_vals, "row", split_axis=0, concat_axis=1, tiled=True),
        lax.all_to_all(right_vals, "row", split_axis=0, concat_axis=1, tiled=True),
    )


def finish(pair_act, triangle, gate_vals, weights_out):
    tri_normed = layer_norm(triangle.astype(F32), 0).astype(BF16)
    delta_vals = jnp.einsum("crj,cd->rjd", tri_normed, weights_out, preferred_element_type=F32)
    delta_vals = delta_vals * gate_vals.astype(F32)
    return (pair_act.astype(F32) + delta_vals).astype(BF16)


def split_rows(pair_act, in_weights, out_weights, chain_lengths):
    row_tile = pair_act.shape[0]
    col_tile = pair_act.shape[1]
    total_rows = row_tile * lax.axis_size("row")
    count_valid = total_rows - chain_lengths[chain_lengths.shape[0] - 1]
    row_first = lax.axis_index("row") * row_tile
    col_first = lax.axis_index("col") * col_tile
    row_valid = (row_first + jnp.arange(row_tile, dtype=jnp.int32) < count_valid).astype(F32)
    col_valid = (col_first + jnp.arange(col_tile, dtype=jnp.int32) < count_valid).astype(F32)
    pair_mask = row_valid[:, None] * col_valid[None, :]
    left_vals, right_vals, gate_vals = project(pair_act, in_weights[0], pair_mask)
    left_chan, right_chan = to_channels(left_vals, right_vals)
    left_rows = lax.all_to_all(left_chan, "col", split_axis=1, concat_axis=2, tiled=True)
    summed = jnp.einsum(
        "cik,cjk->cij",
        left_rows,
        lax.all_gather(right_chan, "col", axis=2, tiled=True),
        preferred_element_type=F32,
    )
    triangle = lax.all_to_all(
        lax.all_to_all(summed.astype(BF16), "col", split_axis=2, concat_axis=1, tiled=True),
        "row",
        split_axis=1,
        concat_axis=0,
        tiled=True,
    )
    first_pass = finish(pair_act, triangle, gate_vals, out_weights[0])
    left_vals, right_vals, gate_vals = project(first_pass, in_weights[1], pair_mask)
    left_chan, right_chan = to_channels(left_vals, right_vals)
    summed_in = jnp.einsum(
        "cki,ckj->cij",
        lax.all_gather(left_chan, "col", axis=2, tiled=True),
        right_chan,
        preferred_element_type=F32,
    ).astype(BF16)
    triangle_in = lax.all_to_all(summed_in, "row", split_axis=1, concat_axis=0, tiled=True)
    return finish(first_pass, triangle_in, gate_vals, out_weights[1])


def solution(mesh):
    n_parts, n_row, n_col = (mesh.shape[axis] for axis in ("parts", "row", "col"))

    def by_rows(pair_act, in_weights, out_weights, chain_lengths):
        in_specs = (P(("parts", "row"), "col", None), P(), P(), P("parts"))
        return jax.shard_map(
            split_rows, mesh=mesh, in_specs=in_specs, out_specs=in_specs[0], check_vma=False
        )(pair_act, in_weights, out_weights, chain_lengths)

    def by_channels(pair_act, in_weights, out_weights, chain_lengths):
        halves = jax.sharding.Mesh(
            mesh.devices.reshape(n_parts, 2, n_row // 2, n_col), ("parts", "half", "row", "col")
        )
        in_specs = (P(("parts", "half", "row"), "col", None), P(), P(), P("parts"))
        return jax.shard_map(
            functools.partial(split_channels, 2, n_row // 2, n_col),
            mesh=halves, in_specs=in_specs, out_specs=in_specs[0], check_vma=False,
        )(pair_act, in_weights, out_weights, chain_lengths)

    def program(pair_act, in_weights, out_weights, chain_lengths):
        fits = n_row % 2 == 0 and pair_act.shape[2] % (n_row * n_col) == 0
        form = by_channels if fits else by_rows
        return form(pair_act, in_weights, out_weights, chain_lengths)

    return program
```

```python
import functools
import itertools

import jax
import jax.numpy as jnp
from jax import lax
from jax.experimental import pallas as pl
from jax.experimental.pallas import tpu as pltpu
from jax.sharding import PartitionSpec as P

epsilon = 1e-05
F32 = jnp.float32
BF16 = jnp.bfloat16
VMEM_LIMIT = 32 * 1024 * 1024
FIRST_VMEM_LIMIT = 56 * 1024 * 1024
ROW_AXES = ("row_a", "row_b", "row_c", "row_d")
SIDES_ORDER = ("col", "row_d", "row_c", "row_a", "row_b")
TRIANGLE_ORDER = ("col", "row_c", "row_b", "row_d", "row_a")


def layer_norm(values, along_axis):
    mean_vals = jnp.mean(values, axis=along_axis, keepdims=True)
    centred = values - mean_vals
    variance = jnp.mean(centred * centred, axis=along_axis, keepdims=True)
    return centred * lax.rsqrt(variance + epsilon)


def sigmoid(values):
    return 0.5 * jnp.tanh(0.5 * values) + 0.5


def dot(lhs, rhs):
    return jnp.dot(lhs, rhs, preferred_element_type=F32)


def store_mask(ref, row_limit, col_limit):
    row = lax.broadcasted_iota(jnp.int32, ref.shape, 0)
    col = lax.broadcasted_iota(jnp.int32, ref.shape, 1)
    ref[...] = jnp.where(jnp.logical_and(row < row_limit, col < col_limit), 1.0, 0.0).astype(F32)


def load_mask(ref, first, group):
    return jnp.concatenate([ref[first + g : first + g + 1, :] for g in range(group)], axis=1)


def store_rows(ref, first, group, vals):
    cols = vals.shape[1] // group
    for g in range(group):
        ref[first + g] = vals[:, g * cols : (g + 1) * cols]


def load_rows(ref, first, group):
    return jnp.concatenate([ref[first + g] for g in range(group)], axis=1)


def project_rows(first, group, pair_vals, mask, weights_t, left_scr, right_scr, gate_ref):
    width = pair_vals.shape[0]
    normed = layer_norm(pair_vals, 0).astype(BF16)
    for side, scr in enumerate((left_scr, right_scr)):
        both = dot(weights_t[2 * side * width : (2 * side + 2) * width, :], normed)
        vals = sigmoid(both[0:width]) * both[width : 2 * width] * mask
        store_rows(scr, first, group, vals.astype(BF16))
    gate = sigmoid(dot(weights_t[4 * width : 5 * width, :], normed))
    store_rows(gate_ref, first, group, gate.astype(BF16))


def send_channels(blocks, left_scr, right_scr, send_ref):
    per = send_ref.shape[2]
    for side, scr in enumerate((left_scr, right_scr)):
        swapped = jnp.swapaxes(scr[...], 0, 1)
        for place, block in enumerate(blocks):
            send_ref[place, side] = swapped[block * per : (block + 1) * per]


def first_kernel(
    blocks, lengths_hbm, pair_hbm, weights_hbm, send_ref, gate_ref, pair_t_ref, mask_ref,
    left_scr, right_scr, wt_scr, lengths_scr, pair_scr, weights_scr, sems,
):
    rows, cols, width = pair_scr.shape
    group = 2
    fetches = [
        pltpu.make_async_copy(weights_hbm.at[0], weights_scr, sems.at[0]),
        pltpu.make_async_copy(pair_hbm, pair_scr, sems.at[1]),
        pltpu.make_async_copy(lengths_hbm, lengths_scr, sems.at[2]),
    ]
    for fetch in fetches:
        fetch.start()
    for fetch in fetches:
        fetch.wait()
    valid = rows * lax.axis_size(ROW_AXES) - lengths_scr[lengths_scr.shape[0] - 1]
    row_first = functools.reduce(lambda at, axis: at * lax.axis_size(axis) + lax.axis_index(axis), ROW_AXES, 0)
    store_mask(mask_ref, valid - row_first * rows, valid - lax.axis_index("col") * cols)
    wt_scr[...] = weights_scr[...].T
    for first in range(0, rows, group):
        pair = jnp.concatenate([pair_scr[first + g].T for g in range(group)], axis=1)
        store_rows(pair_t_ref, first, group, pair)
        project_rows(
            first, group, pair.astype(F32), load_mask(mask_ref, first, group),
            wt_scr, left_scr, right_scr, gate_ref,
        )
    send_channels(blocks, left_scr, right_scr, send_ref)


def finish_rows(first, group, tri_scr, wo_t, gate_ref, pair_t_ref):
    tri = load_rows(tri_scr, first, group).astype(F32)
    delta = dot(wo_t, layer_norm(tri, 0).astype(BF16))
    gate = load_rows(gate_ref, first, group).astype(F32)
    return (load_rows(pair_t_ref, first, group).astype(F32) + delta * gate).astype(BF16)


def middle_kernel(
    blocks, tri_ref, gate_in_ref, pair_t_in_ref, mask_ref, wo_ref, weights_ref,
    send_ref, gate_ref, pair_t_ref, left_scr, right_scr, wt_scr, tri_scr,
):
    width, rows, cols = tri_ref.shape
    group = 2
    wt_scr[...] = weights_ref[1].T
    wo_t = wo_ref[0].T
    tri_scr[...] = jnp.swapaxes(tri_ref[...], 0, 1)
    for first in range(0, rows, group):
        passed = finish_rows(first, group, tri_scr, wo_t, gate_in_ref, pair_t_in_ref)
        store_rows(pair_t_ref, first, group, passed)
        project_rows(
            first, group, passed.astype(F32), load_mask(mask_ref, first, group),
            wt_scr, left_scr, right_scr, gate_ref,
        )
    send_channels(blocks, left_scr, right_scr, send_ref)


def last_kernel(tri_ref, gate_ref, pair_t_ref, wo_ref, out_ref, tri_scr):
    width, rows, cols = tri_ref.shape
    group = 2
    wo_t = wo_ref[1].T
    tri_scr[...] = jnp.swapaxes(tri_ref[...], 0, 1)
    for first in range(0, rows, group):
        passed = finish_rows(first, group, tri_scr, wo_t, gate_ref, pair_t_ref)
        for g in range(group):
            out_ref[first + g] = passed[:, g * cols : (g + 1) * cols].T


def triangle_kernel(incoming, places, out_places, recv_ref, out_ref):
    _, _, per, rows, cols = recv_ref.shape
    for c in range(per):
        left, right = (
            jnp.concatenate(
                [jnp.concatenate([recv_ref[p, side, c] for p in column], axis=0) for column in places], axis=1
            )
            for side in (0, 1)
        )
        dims = (((0,), (0,)), ((), ())) if incoming else (((1,), (1,)), ((), ()))
        tri = lax.dot_general(left, right, dims, preferred_element_type=F32).astype(BF16)
        for x, column in enumerate(out_places):
            for r, p in enumerate(column):
                out_ref[p, c] = tri[r * rows : (r + 1) * rows, x * cols : (x + 1) * cols]


def call(kernel, name, out_shape, scratch, in_specs, flops, *args, vmem=VMEM_LIMIT):
    return pl.pallas_call(
        kernel,
        name=name,
        out_shape=out_shape,
        in_specs=in_specs,
        out_specs=jax.tree.map(lambda _: pl.BlockSpec(memory_space=pltpu.VMEM), out_shape),
        scratch_shapes=scratch,
        compiler_params=pltpu.CompilerParams(vmem_limit_bytes=vmem),
        cost_estimate=pl.CostEstimate(flops=flops, bytes_accessed=2 << 20, transcendentals=0),
    )(*args)


VM = pl.BlockSpec(memory_space=pltpu.VMEM)
HBM = pl.BlockSpec(memory_space=pltpu.HBM)


def places_of(sizes, order):
    places = {}
    for place, index in enumerate(itertools.product(*(range(sizes[axis]) for axis in order))):
        at = dict(zip(order, index))
        row = 0
        for axis in ROW_AXES:
            row = row * sizes[axis] + at[axis]
        places[at["col"], row] = place
    n_col, n_row = sizes["col"], len(places) // sizes["col"]
    return [[places[x, r] for r in range(n_row)] for x in range(n_col)]


def split_channels(sizes, pair_act, in_weights, out_weights, chain_lengths):
    rows, cols, width = pair_act.shape
    places, out_places = places_of(sizes, SIDES_ORDER), places_of(sizes, TRIANGLE_ORDER)
    group = len(places) * len(places[0])
    per = width // group
    owner = {p: q for col, out_col in zip(places, out_places) for p, q in zip(col, out_col)}
    blocks = [owner[p] for p in range(group)]

    send_shape = jax.ShapeDtypeStruct((group, 2, per, rows, cols), BF16)
    block_shape = jax.ShapeDtypeStruct((rows, width, cols), BF16)
    tri_shape = jax.ShapeDtypeStruct((group, per, rows, cols), BF16)
    scr = pltpu.VMEM((rows, width, cols), BF16)
    wt_scr = pltpu.VMEM((5 * width, width), BF16)
    flops_in = 2 * rows * cols * width * 5 * width
    flops_out = 2 * rows * cols * width * width
    flops_tri = 2 * group * rows * cols * width * rows * len(places[0])

    def exchange(array, order):
        return lax.all_to_all(array, order, split_axis=0, concat_axis=0, tiled=True)

    def triangle(send, incoming):
        kernel = functools.partial(triangle_kernel, incoming, places, out_places)
        recv = exchange(send, SIDES_ORDER)
        tri = call(kernel, "triangle", tri_shape, [], [VM], flops_tri, recv)
        return exchange(tri, TRIANGLE_ORDER).reshape(width, rows, cols)

    send, gate, pair_t, mask = call(
        functools.partial(first_kernel, blocks), "project",
        (send_shape, block_shape, block_shape, jax.ShapeDtypeStruct((rows, cols), F32)),
        [
            scr, scr, wt_scr, pltpu.SMEM(chain_lengths.shape, jnp.int32), pltpu.VMEM(pair_act.shape, BF16),
            pltpu.VMEM(in_weights.shape[1:], BF16), pltpu.SemaphoreType.DMA((3,)),
        ],
        [HBM, HBM, HBM], flops_in, chain_lengths, pair_act, in_weights, vmem=FIRST_VMEM_LIMIT,
    )
    tri = triangle(send, False)
    send, gate, pair_t = call(
        functools.partial(middle_kernel, blocks), "finish_project", (send_shape, block_shape, block_shape),
        [scr, scr, wt_scr, scr], [VM] * 6, flops_in + flops_out,
        tri, gate, pair_t, mask, out_weights, in_weights,
    )
    tri = triangle(send, True)
    return call(
        last_kernel, "finish", jax.ShapeDtypeStruct(pair_act.shape, BF16), [scr],
        [VM, VM, VM, VM], flops_out, tri, gate, pair_t, out_weights,
    )


def project(pair_act, weights, pair_mask):
    width = pair_act.shape[2]
    normed = layer_norm(pair_act.astype(F32), 2).astype(BF16)
    projected = jnp.einsum("rjd,de->erj", normed, weights[:, 0 : 4 * width], preferred_element_type=F32)
    left_vals = (jax.nn.sigmoid(projected[0:width]) * projected[width : 2 * width] * pair_mask).astype(BF16)
    right_vals = (
        jax.nn.sigmoid(projected[2 * width : 3 * width]) * projected[3 * width : 4 * width] * pair_mask
    ).astype(BF16)
    gate_vals = jax.nn.sigmoid(
        jnp.einsum("rjd,de->rje", normed, weights[:, 4 * width : 5 * width], preferred_element_type=F32)
    ).astype(BF16)
    return (left_vals, right_vals, gate_vals)


def to_channels(left_vals, right_vals):
    return (
        lax.all_to_all(left_vals, "row", split_axis=0, concat_axis=1, tiled=True),
        lax.all_to_all(right_vals, "row", split_axis=0, concat_axis=1, tiled=True),
    )


def finish(pair_act, triangle, gate_vals, weights_out):
    tri_normed = layer_norm(triangle.astype(F32), 0).astype(BF16)
    delta_vals = jnp.einsum("crj,cd->rjd", tri_normed, weights_out, preferred_element_type=F32)
    delta_vals = delta_vals * gate_vals.astype(F32)
    return (pair_act.astype(F32) + delta_vals).astype(BF16)


def split_rows(pair_act, in_weights, out_weights, chain_lengths):
    row_tile = pair_act.shape[0]
    col_tile = pair_act.shape[1]
    total_rows = row_tile * lax.axis_size("row")
    count_valid = total_rows - chain_lengths[chain_lengths.shape[0] - 1]
    row_first = lax.axis_index("row") * row_tile
    col_first = lax.axis_index("col") * col_tile
    row_valid = (row_first + jnp.arange(row_tile, dtype=jnp.int32) < count_valid).astype(F32)
    col_valid = (col_first + jnp.arange(col_tile, dtype=jnp.int32) < count_valid).astype(F32)
    pair_mask = row_valid[:, None] * col_valid[None, :]
    left_vals, right_vals, gate_vals = project(pair_act, in_weights[0], pair_mask)
    left_chan, right_chan = to_channels(left_vals, right_vals)
    left_rows = lax.all_to_all(left_chan, "col", split_axis=1, concat_axis=2, tiled=True)
    summed = jnp.einsum(
        "cik,cjk->cij",
        left_rows,
        lax.all_gather(right_chan, "col", axis=2, tiled=True),
        preferred_element_type=F32,
    )
    triangle = lax.all_to_all(
        lax.all_to_all(summed.astype(BF16), "col", split_axis=2, concat_axis=1, tiled=True),
        "row",
        split_axis=1,
        concat_axis=0,
        tiled=True,
    )
    first_pass = finish(pair_act, triangle, gate_vals, out_weights[0])
    left_vals, right_vals, gate_vals = project(first_pass, in_weights[1], pair_mask)
    left_chan, right_chan = to_channels(left_vals, right_vals)
    summed_in = jnp.einsum(
        "cki,ckj->cij",
        lax.all_gather(left_chan, "col", axis=2, tiled=True),
        right_chan,
        preferred_element_type=F32,
    ).astype(BF16)
    triangle_in = lax.all_to_all(summed_in, "row", split_axis=1, concat_axis=0, tiled=True)
    return finish(first_pass, triangle_in, gate_vals, out_weights[1])


def solution(mesh):
    n_parts, n_row, n_col = (mesh.shape[axis] for axis in ("parts", "row", "col"))

    def by_rows(*args):
        in_specs = (P(("parts", "row"), "col", None), P(), P(), P("parts"))
        return jax.shard_map(
            split_rows, mesh=mesh, in_specs=in_specs, out_specs=in_specs[0], check_vma=False
        )(*args)

    def by_channels(*args):
        shape = (n_parts, n_row // 8, 2, 2, 2, n_col)
        axes = ("parts",) + ROW_AXES + ("col",)
        fine = jax.sharding.Mesh(mesh.devices.reshape(shape), axes)
        in_specs = (P(axes[:-1], "col", None), P(), P(), P("parts"))
        return jax.shard_map(
            functools.partial(split_channels, dict(zip(axes, shape))),
            mesh=fine, in_specs=in_specs, out_specs=in_specs[0], check_vma=False,
        )(*args)

    def program(pair_act, in_weights, out_weights, chain_lengths):
        fits = n_row % 8 == 0 and pair_act.shape[2] % (n_row * n_col) == 0
        form = by_channels if fits else by_rows
        return form(pair_act, in_weights, out_weights, chain_lengths)

    return program
```

```python
import functools
import itertools

import jax
import jax.numpy as jnp
from jax import lax
from jax.experimental import pallas as pl
from jax.experimental.pallas import tpu as pltpu
from jax.sharding import PartitionSpec as P

epsilon = 1e-05
F32 = jnp.float32
BF16 = jnp.bfloat16
VMEM_LIMIT = 32 * 1024 * 1024
FIRST_VMEM_LIMIT = 56 * 1024 * 1024
ROW_AXES = ("row_a", "row_b", "row_c", "row_d")
RIGHT_ORDER = ("col", "row_d", "row_a", "row_c", "row_b")
SIDES_ORDER = ("col", "row_d", "row_c", "row_a", "row_b")
TRIANGLE_ORDER = ("col", "row_c", "row_b", "row_d", "row_a")
HALF_ORDER = ("row_c", "col", "row_d", "row_b")
FLIPS = ((0, 0), (0, 1), (1, 0), (1, 1))


def layer_norm(values, along_axis):
    mean_vals = jnp.mean(values, axis=along_axis, keepdims=True)
    centred = values - mean_vals
    variance = jnp.mean(centred * centred, axis=along_axis, keepdims=True)
    return centred * lax.rsqrt(variance + epsilon)


def sigmoid(values):
    return 0.5 * jnp.tanh(0.5 * values) + 0.5


def dot(lhs, rhs):
    return jnp.dot(lhs, rhs, preferred_element_type=F32)


def store_mask(ref, row_limit, col_limit):
    row = lax.broadcasted_iota(jnp.int32, ref.shape, 0)
    col = lax.broadcasted_iota(jnp.int32, ref.shape, 1)
    ref[...] = jnp.where(jnp.logical_and(row < row_limit, col < col_limit), 1.0, 0.0).astype(F32)


def load_mask(ref, first, group):
    return jnp.concatenate([ref[first + g : first + g + 1, :] for g in range(group)], axis=1)


def store_rows(ref, first, group, vals):
    cols = vals.shape[1] // group
    for g in range(group):
        ref[first + g] = vals[:, g * cols : (g + 1) * cols]


def load_rows(ref, first, group):
    return jnp.concatenate([ref[first + g] for g in range(group)], axis=1)


def project_rows(first, group, pair_vals, mask, weights_t, left_scr, right_scr, gate_ref):
    width = pair_vals.shape[0]
    normed = layer_norm(pair_vals, 0).astype(BF16)
    for side, scr in enumerate((left_scr, right_scr)):
        both = dot(weights_t[2 * side * width : (2 * side + 2) * width, :], normed)
        vals = sigmoid(both[0:width]) * both[width : 2 * width] * mask
        store_rows(scr, first, group, vals.astype(BF16))
    gate = sigmoid(dot(weights_t[4 * width : 5 * width, :], normed))
    store_rows(gate_ref, first, group, gate.astype(BF16))


def send_channels(blocks, left_scr, right_scr, send_ref):
    per = send_ref.shape[2]
    for side, scr in enumerate((left_scr, right_scr)):
        swapped = jnp.swapaxes(scr[...], 0, 1)
        for place, block in enumerate(blocks):
            send_ref[place, side] = swapped[block * per : (block + 1) * per]


def half_place(col, row_c, row_b, row_d):
    at = {"col": col, "row_c": row_c, "row_b": row_b, "row_d": row_d}
    return functools.reduce(lambda place, axis: 2 * place + at[axis], HALF_ORDER, 0)


def flip(axis, by):
    at = lax.axis_index(axis)
    return 1 - at if by else at


def first_kernel(
    blocks, lengths_hbm, pair_hbm, weights_hbm, right_ref, own_ref, core_ref, z_ref, z_core_ref,
    gate_ref, pair_t_ref, mask_ref,
    left_scr, right_scr, wt_scr, lengths_scr, pair_scr, weights_scr, owner_scr, sems,
):
    rows, cols, width = pair_scr.shape
    group = 2
    fetches = [
        pltpu.make_async_copy(weights_hbm.at[0], weights_scr, sems.at[0]),
        pltpu.make_async_copy(pair_hbm, pair_scr, sems.at[1]),
        pltpu.make_async_copy(lengths_hbm, lengths_scr, sems.at[2]),
    ]
    for fetch in fetches:
        fetch.start()
    for fetch in fetches:
        fetch.wait()
    valid = rows * lax.axis_size(ROW_AXES) - lengths_scr[lengths_scr.shape[0] - 1]
    row_first = functools.reduce(lambda at, axis: at * lax.axis_size(axis) + lax.axis_index(axis), ROW_AXES, 0)
    store_mask(mask_ref, valid - row_first * rows, valid - lax.axis_index("col") * cols)
    wt_scr[...] = weights_scr[...].T
    for first in range(0, rows, group):
        pair = jnp.concatenate([pair_scr[first + g].T for g in range(group)], axis=1)
        store_rows(pair_t_ref, first, group, pair)
        project_rows(
            first, group, pair.astype(F32), load_mask(mask_ref, first, group),
            wt_scr, left_scr, right_scr, gate_ref,
        )
    per = right_ref.shape[1]
    swapped = jnp.swapaxes(right_scr[...], 0, 1)
    for place, block in enumerate(blocks):
        right_ref[place] = swapped[block * per : (block + 1) * per]
    owner_scr[...] = jnp.swapaxes(left_scr[...], 0, 1).reshape(owner_scr.shape)
    for part_ref, (by_z, by_core) in zip((own_ref, core_ref, z_ref, z_core_ref), FLIPS):
        for x_y in range(4):
            part_ref[x_y] = owner_scr[half_place(x_y // 2, x_y % 2, flip("row_b", by_z), flip("row_d", by_core))]


def regroup_kernel(*refs):
    for part_ref, (by_y, by_x) in zip(refs[4:], FLIPS):
        at = flip("col", by_x) * 2 + flip("row_c", by_y)
        for sender in range(4):
            part_ref[sender] = refs[sender][at]


def finish_rows(first, group, tri_scr, wo_t, gate_ref, pair_t_ref):
    tri = load_rows(tri_scr, first, group).astype(F32)
    delta = dot(wo_t, layer_norm(tri, 0).astype(BF16))
    gate = load_rows(gate_ref, first, group).astype(F32)
    return (load_rows(pair_t_ref, first, group).astype(F32) + delta * gate).astype(BF16)


def middle_kernel(
    blocks, tri_ref, gate_in_ref, pair_t_in_ref, mask_ref, wo_ref, weights_ref,
    send_ref, gate_ref, pair_t_ref, left_scr, right_scr, wt_scr, tri_scr,
):
    width, rows, cols = tri_ref.shape
    group = 2
    wt_scr[...] = weights_ref[1].T
    wo_t = wo_ref[0].T
    tri_scr[...] = jnp.swapaxes(tri_ref[...], 0, 1)
    for first in range(0, rows, group):
        passed = finish_rows(first, group, tri_scr, wo_t, gate_in_ref, pair_t_in_ref)
        store_rows(pair_t_ref, first, group, passed)
        project_rows(
            first, group, passed.astype(F32), load_mask(mask_ref, first, group),
            wt_scr, left_scr, right_scr, gate_ref,
        )
    send_channels(blocks, left_scr, right_scr, send_ref)


def last_kernel(tri_ref, gate_ref, pair_t_ref, wo_ref, out_ref, tri_scr):
    width, rows, cols = tri_ref.shape
    group = 2
    wo_t = wo_ref[1].T
    tri_scr[...] = jnp.swapaxes(tri_ref[...], 0, 1)
    for first in range(0, rows, group):
        passed = finish_rows(first, group, tri_scr, wo_t, gate_ref, pair_t_ref)
        for g in range(group):
            out_ref[first + g] = passed[:, g * cols : (g + 1) * cols].T


def outgoing_kernel(places, *refs):
    left_refs, (right_ref, out_ref) = refs[:4], refs[4:]
    _, per, rows, cols = right_ref.shape
    first_col = lax.axis_index("col") == 0
    deltas = [(z_core, by_y) for z_core in range(4) for by_y in range(2)]
    for c in range(per):
        same, across = (
            jnp.concatenate([left_refs[2 * by_y + by_x][z_core, c] for z_core, by_y in deltas], axis=0)
            for by_x in (0, 1)
        )
        left = jnp.concatenate(
            [jnp.where(first_col, same, across), jnp.where(first_col, across, same)], axis=1
        )
        right = jnp.concatenate(
            [jnp.concatenate([right_ref[p, c] for p in column], axis=0) for column in places], axis=1
        )
        tri = lax.dot_general(
            left, right, (((1,), (1,)), ((), ())), preferred_element_type=F32
        ).astype(BF16)
        for block, (z_core, by_y) in enumerate(deltas):
            by_z, by_core = FLIPS[z_core]
            at = flip("row_c", by_y), flip("row_b", by_z), flip("row_d", by_core)
            for x in range(len(places)):
                out_ref[half_place(x, *at), c] = tri[block * rows : (block + 1) * rows, x * cols : (x + 1) * cols]


def incoming_kernel(places, out_places, recv_ref, out_ref):
    _, _, per, rows, cols = recv_ref.shape
    for c in range(per):
        left, right = (
            jnp.concatenate(
                [jnp.concatenate([recv_ref[p, side, c] for p in column], axis=0) for column in places], axis=1
            )
            for side in (0, 1)
        )
        tri = lax.dot_general(
            left, right, (((0,), (0,)), ((), ())), preferred_element_type=F32
        ).astype(BF16)
        for x, column in enumerate(out_places):
            for r, p in enumerate(column):
                out_ref[p, c] = tri[r * rows : (r + 1) * rows, x * cols : (x + 1) * cols]


def call(kernel, name, out_shape, scratch, in_specs, flops, *args, vmem=VMEM_LIMIT):
    return pl.pallas_call(
        kernel,
        name=name,
        out_shape=out_shape,
        in_specs=in_specs,
        out_specs=jax.tree.map(lambda _: pl.BlockSpec(memory_space=pltpu.VMEM), out_shape),
        scratch_shapes=scratch,
        compiler_params=pltpu.CompilerParams(vmem_limit_bytes=vmem),
        cost_estimate=pl.CostEstimate(flops=flops, bytes_accessed=2 << 20, transcendentals=0),
    )(*args)


VM = pl.BlockSpec(memory_space=pltpu.VMEM)
HBM = pl.BlockSpec(memory_space=pltpu.HBM)


def places_of(sizes, order):
    places = {}
    for place, index in enumerate(itertools.product(*(range(sizes[axis]) for axis in order))):
        at = dict(zip(order, index))
        row = 0
        for axis in ROW_AXES:
            row = row * sizes[axis] + at[axis]
        places[at["col"], row] = place
    n_col, n_row = sizes["col"], len(places) // sizes["col"]
    return [[places[x, r] for r in range(n_row)] for x in range(n_col)]


def to_partners(parts, axes):
    pairs = [[(0, 1), (1, 0)], [(0, 1), (1, 0)], [(0, 3), (1, 2), (2, 1), (3, 0)]]
    names = (axes[1], axes[0], axes)
    return [parts[0]] + [lax.ppermute(p, name, pair) for p, name, pair in zip(parts[1:], names, pairs)]


def split_channels(sizes, pair_act, in_weights, out_weights, chain_lengths):
    rows, cols, width = pair_act.shape
    places, out_places = places_of(sizes, SIDES_ORDER), places_of(sizes, TRIANGLE_ORDER)
    n_col, n_row = len(places), len(places[0])
    group, half_group = n_col * n_row, n_col * n_row // 2
    per, half_per = width // group, width // half_group
    owner = {p: q for col, out_col in zip(places, out_places) for p, q in zip(col, out_col)}
    blocks = [owner[p] for p in range(group)]
    right_places = places_of(sizes, RIGHT_ORDER)
    half_places = places_of({**sizes, "row_a": 1}, HALF_ORDER + ("row_a",))
    half_owner = {p: q for col, half_col in zip(right_places, half_places) for p, q in zip(col, half_col * 2)}
    half_blocks = [half_owner[p] for p in range(group)]

    def shape_of(*dims, dtype=BF16):
        return jax.ShapeDtypeStruct(dims, dtype)

    block_shape = shape_of(rows, width, cols)
    part_shape = shape_of(4, half_per, rows, cols)
    scr = pltpu.VMEM((rows, width, cols), BF16)
    wt_scr = pltpu.VMEM((5 * width, width), BF16)
    flops_in = 2 * rows * cols * width * 5 * width
    flops_out = 2 * rows * cols * width * width
    flops_tri = 2 * group * rows * cols * width * rows * n_row

    def exchange(array, order):
        return lax.all_to_all(array, order, split_axis=0, concat_axis=0, tiled=True)

    right, *left, gate, pair_t, mask = call(
        functools.partial(first_kernel, half_blocks), "project",
        (shape_of(group, half_per, rows, cols),) + (part_shape,) * 4
        + (block_shape, block_shape, shape_of(rows, cols, dtype=F32)),
        [
            scr, scr, wt_scr, pltpu.SMEM(chain_lengths.shape, jnp.int32), pltpu.VMEM(pair_act.shape, BF16),
            pltpu.VMEM(in_weights.shape[1:], BF16), pltpu.VMEM((half_group, half_per, rows, cols), BF16),
            pltpu.SemaphoreType.DMA((3,)),
        ],
        [HBM, HBM, HBM], flops_in, chain_lengths, pair_act, in_weights, vmem=FIRST_VMEM_LIMIT,
    )
    right = exchange(right, RIGHT_ORDER)
    left = to_partners(left, ("row_b", "row_d"))
    left = call(regroup_kernel, "regroup", (part_shape,) * 4, [], [VM] * 4, 3000 * flops_out, *left, vmem=4 * 1024 * 1024)
    left = to_partners(left, ("row_c", "col"))
    tri = call(
        functools.partial(outgoing_kernel, right_places), "outgoing", shape_of(half_group, half_per, rows, cols),
        [], [VM] * 5, flops_tri, *left, right,
    )
    tri = exchange(tri, HALF_ORDER).reshape(width, rows, cols)
    send, gate, pair_t = call(
        functools.partial(middle_kernel, blocks), "finish_project",
        (shape_of(group, 2, per, rows, cols), block_shape, block_shape),
        [scr, scr, wt_scr, scr], [VM] * 6, flops_in + flops_out,
        tri, gate, pair_t, mask, out_weights, in_weights,
    )
    recv = exchange(send, SIDES_ORDER)
    tri = call(
        functools.partial(incoming_kernel, places, out_places), "incoming", shape_of(group, per, rows, cols),
        [], [VM], flops_tri, recv,
    )
    tri = exchange(tri, TRIANGLE_ORDER).reshape(width, rows, cols)
    return call(
        last_kernel, "finish", shape_of(*pair_act.shape), [scr],
        [VM, VM, VM, VM], flops_out, tri, gate, pair_t, out_weights,
    )


def project(pair_act, weights, pair_mask):
    width = pair_act.shape[2]
    normed = layer_norm(pair_act.astype(F32), 2).astype(BF16)
    projected = jnp.einsum("rjd,de->erj", normed, weights[:, 0 : 4 * width], preferred_element_type=F32)
    left_vals = (jax.nn.sigmoid(projected[0:width]) * projected[width : 2 * width] * pair_mask).astype(BF16)
    right_vals = (
        jax.nn.sigmoid(projected[2 * width : 3 * width]) * projected[3 * width : 4 * width] * pair_mask
    ).astype(BF16)
    gate_vals = jax.nn.sigmoid(
        jnp.einsum("rjd,de->rje", normed, weights[:, 4 * width : 5 * width], preferred_element_type=F32)
    ).astype(BF16)
    return (left_vals, right_vals, gate_vals)


def to_channels(left_vals, right_vals):
    return (
        lax.all_to_all(left_vals, "row", split_axis=0, concat_axis=1, tiled=True),
        lax.all_to_all(right_vals, "row", split_axis=0, concat_axis=1, tiled=True),
    )


def finish(pair_act, triangle, gate_vals, weights_out):
    tri_normed = layer_norm(triangle.astype(F32), 0).astype(BF16)
    delta_vals = jnp.einsum("crj,cd->rjd", tri_normed, weights_out, preferred_element_type=F32)
    delta_vals = delta_vals * gate_vals.astype(F32)
    return (pair_act.astype(F32) + delta_vals).astype(BF16)


def split_rows(pair_act, in_weights, out_weights, chain_lengths):
    row_tile = pair_act.shape[0]
    col_tile = pair_act.shape[1]
    total_rows = row_tile * lax.axis_size("row")
    count_valid = total_rows - chain_lengths[chain_lengths.shape[0] - 1]
    row_first = lax.axis_index("row") * row_tile
    col_first = lax.axis_index("col") * col_tile
    row_valid = (row_first + jnp.arange(row_tile, dtype=jnp.int32) < count_valid).astype(F32)
    col_valid = (col_first + jnp.arange(col_tile, dtype=jnp.int32) < count_valid).astype(F32)
    pair_mask = row_valid[:, None] * col_valid[None, :]
    left_vals, right_vals, gate_vals = project(pair_act, in_weights[0], pair_mask)
    left_chan, right_chan = to_channels(left_vals, right_vals)
    left_rows = lax.all_to_all(left_chan, "col", split_axis=1, concat_axis=2, tiled=True)
    summed = jnp.einsum(
        "cik,cjk->cij",
        left_rows,
        lax.all_gather(right_chan, "col", axis=2, tiled=True),
        preferred_element_type=F32,
    )
    triangle = lax.all_to_all(
        lax.all_to_all(summed.astype(BF16), "col", split_axis=2, concat_axis=1, tiled=True),
        "row",
        split_axis=1,
        concat_axis=0,
        tiled=True,
    )
    first_pass = finish(pair_act, triangle, gate_vals, out_weights[0])
    left_vals, right_vals, gate_vals = project(first_pass, in_weights[1], pair_mask)
    left_chan, right_chan = to_channels(left_vals, right_vals)
    summed_in = jnp.einsum(
        "cki,ckj->cij",
        lax.all_gather(left_chan, "col", axis=2, tiled=True),
        right_chan,
        preferred_element_type=F32,
    ).astype(BF16)
    triangle_in = lax.all_to_all(summed_in, "row", split_axis=1, concat_axis=0, tiled=True)
    return finish(first_pass, triangle_in, gate_vals, out_weights[1])


def solution(mesh):
    n_parts, n_row, n_col = (mesh.shape[axis] for axis in ("parts", "row", "col"))

    def by_rows(*args):
        in_specs = (P(("parts", "row"), "col", None), P(), P(), P("parts"))
        return jax.shard_map(
            split_rows, mesh=mesh, in_specs=in_specs, out_specs=in_specs[0], check_vma=False
        )(*args)

    def by_channels(*args):
        shape = (n_parts, n_row // 8, 2, 2, 2, n_col)
        axes = ("parts",) + ROW_AXES + ("col",)
        fine = jax.sharding.Mesh(mesh.devices.reshape(shape), axes)
        in_specs = (P(axes[:-1], "col", None), P(), P(), P("parts"))
        return jax.shard_map(
            functools.partial(split_channels, dict(zip(axes, shape))),
            mesh=fine, in_specs=in_specs, out_specs=in_specs[0], check_vma=False,
        )(*args)

    def program(pair_act, in_weights, out_weights, chain_lengths):
        fits = n_row == 16 and n_col == 2 and pair_act.shape[2] % 32 == 0
        form = by_channels if fits else by_rows
        return form(pair_act, in_weights, out_weights, chain_lengths)

    return program
```

```python
import functools
import itertools

import jax
import jax.numpy as jnp
from jax import lax
from jax.experimental import pallas as pl
from jax.experimental.pallas import tpu as pltpu
from jax.sharding import PartitionSpec as P

epsilon = 1e-05
F32 = jnp.float32
BF16 = jnp.bfloat16
VMEM_LIMIT = 32 * 1024 * 1024
FIRST_VMEM_LIMIT = 56 * 1024 * 1024
ROW_AXES = ("row_a", "row_b", "row_c", "row_d")
RIGHT_ORDER = ("col", "row_d", "row_a", "row_c", "row_b")
SIDES_ORDER = ("col", "row_d", "row_c", "row_a", "row_b")
TRIANGLE_ORDER = ("col", "row_c", "row_b", "row_d", "row_a")
HALF_ORDER = ("row_c", "col", "row_d", "row_b")
FLIPS = ((0, 0), (0, 1), (1, 0), (1, 1))


def layer_norm(values, along_axis):
    mean_vals = jnp.mean(values, axis=along_axis, keepdims=True)
    centred = values - mean_vals
    variance = jnp.mean(centred * centred, axis=along_axis, keepdims=True)
    return centred * lax.rsqrt(variance + epsilon)


def sigmoid(values):
    return 0.5 * jnp.tanh(0.5 * values) + 0.5


def dot(lhs, rhs):
    return jnp.dot(lhs, rhs, preferred_element_type=F32)


def store_mask(ref, row_limit, col_limit):
    row = lax.broadcasted_iota(jnp.int32, ref.shape, 0)
    col = lax.broadcasted_iota(jnp.int32, ref.shape, 1)
    ref[...] = jnp.where(jnp.logical_and(row < row_limit, col < col_limit), 1.0, 0.0).astype(F32)


def load_mask(ref, first, group):
    return jnp.concatenate([ref[first + g : first + g + 1, :] for g in range(group)], axis=1)


def store_rows(ref, first, group, vals):
    cols = vals.shape[1] // group
    for g in range(group):
        ref[first + g] = vals[:, g * cols : (g + 1) * cols]


def load_rows(ref, first, group):
    return jnp.concatenate([ref[first + g] for g in range(group)], axis=1)


def project_side(normed, mask, weights_t, side):
    width = normed.shape[0]
    both = dot(weights_t[2 * side * width : (2 * side + 2) * width, :], normed)
    return (sigmoid(both[0:width]) * both[width : 2 * width] * mask).astype(BF16)


def project_rows(first, group, pair_vals, mask, weights_t, left_scr, right_scr, gate_ref):
    width = pair_vals.shape[0]
    normed = layer_norm(pair_vals, 0).astype(BF16)
    for side, scr in enumerate((left_scr, right_scr)):
        store_rows(scr, first, group, project_side(normed, mask, weights_t, side))
    gate = sigmoid(dot(weights_t[4 * width : 5 * width, :], normed))
    store_rows(gate_ref, first, group, gate.astype(BF16))


def send_channels(blocks, left_scr, right_scr, send_ref):
    per = send_ref.shape[2]
    for side, scr in enumerate((left_scr, right_scr)):
        swapped = jnp.swapaxes(scr[...], 0, 1)
        for place, block in enumerate(blocks):
            send_ref[place, side] = swapped[block * per : (block + 1) * per]


def half_place(col, row_c, row_b, row_d):
    at = {"col": col, "row_c": row_c, "row_b": row_b, "row_d": row_d}
    return functools.reduce(lambda place, axis: 2 * place + at[axis], HALF_ORDER, 0)


def flip(axis, by):
    at = lax.axis_index(axis)
    return 1 - at if by else at


def first_kernel(
    blocks, lengths_hbm, pair_hbm, weights_hbm, right_ref, own_ref, core_ref, z_ref, z_core_ref, mask_ref,
    left_scr, right_scr, wt_scr, lengths_scr, pair_scr, weights_scr, owner_scr, sems,
):
    rows, cols, width = pair_scr.shape
    group = 2
    fetches = [
        pltpu.make_async_copy(weights_hbm.at[0], weights_scr, sems.at[0]),
        pltpu.make_async_copy(pair_hbm, pair_scr, sems.at[1]),
        pltpu.make_async_copy(lengths_hbm, lengths_scr, sems.at[2]),
    ]
    for fetch in fetches:
        fetch.start()
    for fetch in fetches:
        fetch.wait()
    valid = rows * lax.axis_size(ROW_AXES) - lengths_scr[lengths_scr.shape[0] - 1]
    row_first = functools.reduce(lambda at, axis: at * lax.axis_size(axis) + lax.axis_index(axis), ROW_AXES, 0)
    store_mask(mask_ref, valid - row_first * rows, valid - lax.axis_index("col") * cols)
    wt_scr[...] = weights_scr[...].T
    for first in range(0, rows, group):
        pair = jnp.concatenate([pair_scr[first + g].T for g in range(group)], axis=1)
        normed = layer_norm(pair.astype(F32), 0).astype(BF16)
        mask = load_mask(mask_ref, first, group)
        for side, scr in enumerate((left_scr, right_scr)):
            store_rows(scr, first, group, project_side(normed, mask, wt_scr, side))
    per = right_ref.shape[1]
    swapped = jnp.swapaxes(right_scr[...], 0, 1)
    for place, block in enumerate(blocks):
        right_ref[place] = swapped[block * per : (block + 1) * per]
    owner_scr[...] = jnp.swapaxes(left_scr[...], 0, 1).reshape(owner_scr.shape)
    for part_ref, (by_z, by_core) in zip((own_ref, core_ref, z_ref, z_core_ref), FLIPS):
        for x_y in range(4):
            part_ref[x_y] = owner_scr[half_place(x_y // 2, x_y % 2, flip("row_b", by_z), flip("row_d", by_core))]


def gate_kernel(pair_ref, weights_ref, gate_ref, pair_t_ref):
    rows, cols, width = pair_ref.shape
    group = 2
    gate_t = weights_ref[0, :, 4 * width : 5 * width].T
    for first in range(0, rows, group):
        pair = jnp.concatenate([pair_ref[first + g].T for g in range(group)], axis=1)
        store_rows(pair_t_ref, first, group, pair)
        normed = layer_norm(pair.astype(F32), 0).astype(BF16)
        store_rows(gate_ref, first, group, sigmoid(dot(gate_t, normed)).astype(BF16))


def regroup_kernel(*refs):
    for part_ref, (by_y, by_x) in zip(refs[4:], FLIPS):
        at = flip("col", by_x) * 2 + flip("row_c", by_y)
        for sender in range(4):
            part_ref[sender] = refs[sender][at]


def finish_rows(first, group, tri_scr, wo_t, gate_ref, pair_t_ref):
    tri = load_rows(tri_scr, first, group).astype(F32)
    delta = dot(wo_t, layer_norm(tri, 0).astype(BF16))
    gate = load_rows(gate_ref, first, group).astype(F32)
    return (load_rows(pair_t_ref, first, group).astype(F32) + delta * gate).astype(BF16)


def middle_kernel(
    blocks, tri_ref, gate_in_ref, pair_t_in_ref, mask_ref, wo_ref, weights_ref,
    send_ref, gate_ref, pair_t_ref, left_scr, right_scr, wt_scr, tri_scr,
):
    width, rows, cols = tri_ref.shape
    group = 2
    wt_scr[...] = weights_ref[1].T
    wo_t = wo_ref[0].T
    tri_scr[...] = jnp.swapaxes(tri_ref[...], 0, 1)
    for first in range(0, rows, group):
        passed = finish_rows(first, group, tri_scr, wo_t, gate_in_ref, pair_t_in_ref)
        store_rows(pair_t_ref, first, group, passed)
        project_rows(
            first, group, passed.astype(F32), load_mask(mask_ref, first, group),
            wt_scr, left_scr, right_scr, gate_ref,
        )
    send_channels(blocks, left_scr, right_scr, send_ref)


def last_kernel(tri_ref, gate_ref, pair_t_ref, wo_ref, out_ref, tri_scr):
    width, rows, cols = tri_ref.shape
    group = 2
    wo_t = wo_ref[1].T
    tri_scr[...] = jnp.swapaxes(tri_ref[...], 0, 1)
    for first in range(0, rows, group):
        passed = finish_rows(first, group, tri_scr, wo_t, gate_ref, pair_t_ref)
        for g in range(group):
            out_ref[first + g] = passed[:, g * cols : (g + 1) * cols].T


def outgoing_kernel(places, *refs):
    left_refs, right_ref, out_ref = refs[:4], refs[4], refs[6]
    _, per, rows, cols = right_ref.shape
    first_col = lax.axis_index("col") == 0
    deltas = [(z_core, by_y) for z_core in range(4) for by_y in range(2)]
    for c in range(per):
        same, across = (
            jnp.concatenate([left_refs[2 * by_y + by_x][z_core, c] for z_core, by_y in deltas], axis=0)
            for by_x in (0, 1)
        )
        left = jnp.concatenate(
            [jnp.where(first_col, same, across), jnp.where(first_col, across, same)], axis=1
        )
        right = jnp.concatenate(
            [jnp.concatenate([right_ref[p, c] for p in column], axis=0) for column in places], axis=1
        )
        tri = lax.dot_general(
            left, right, (((1,), (1,)), ((), ())), preferred_element_type=F32
        ).astype(BF16)
        for block, (z_core, by_y) in enumerate(deltas):
            by_z, by_core = FLIPS[z_core]
            at = flip("row_c", by_y), flip("row_b", by_z), flip("row_d", by_core)
            for x in range(len(places)):
                out_ref[half_place(x, *at), c] = tri[block * rows : (block + 1) * rows, x * cols : (x + 1) * cols]


def incoming_kernel(places, out_places, recv_ref, out_ref):
    _, _, per, rows, cols = recv_ref.shape
    for c in range(per):
        left, right = (
            jnp.concatenate(
                [jnp.concatenate([recv_ref[p, side, c] for p in column], axis=0) for column in places], axis=1
            )
            for side in (0, 1)
        )
        tri = lax.dot_general(
            left, right, (((0,), (0,)), ((), ())), preferred_element_type=F32
        ).astype(BF16)
        for x, column in enumerate(out_places):
            for r, p in enumerate(column):
                out_ref[p, c] = tri[r * rows : (r + 1) * rows, x * cols : (x + 1) * cols]


def call(kernel, name, out_shape, scratch, in_specs, flops, *args, vmem=VMEM_LIMIT):
    return pl.pallas_call(
        kernel,
        name=name,
        out_shape=out_shape,
        in_specs=in_specs,
        out_specs=jax.tree.map(lambda _: pl.BlockSpec(memory_space=pltpu.VMEM), out_shape),
        scratch_shapes=scratch,
        compiler_params=pltpu.CompilerParams(vmem_limit_bytes=vmem),
        cost_estimate=pl.CostEstimate(flops=flops, bytes_accessed=2 << 20, transcendentals=0),
    )(*args)


VM = pl.BlockSpec(memory_space=pltpu.VMEM)
HBM = pl.BlockSpec(memory_space=pltpu.HBM)
ANY = pl.BlockSpec(memory_space=pl.ANY)


def places_of(sizes, order):
    places = {}
    for place, index in enumerate(itertools.product(*(range(sizes[axis]) for axis in order))):
        at = dict(zip(order, index))
        row = 0
        for axis in ROW_AXES:
            row = row * sizes[axis] + at[axis]
        places[at["col"], row] = place
    n_col, n_row = sizes["col"], len(places) // sizes["col"]
    return [[places[x, r] for r in range(n_row)] for x in range(n_col)]


def to_partners(parts, axes):
    pairs = [[(0, 1), (1, 0)], [(0, 1), (1, 0)], [(0, 3), (1, 2), (2, 1), (3, 0)]]
    names = (axes[1], axes[0], axes)
    return [parts[0]] + [lax.ppermute(p, name, pair) for p, name, pair in zip(parts[1:], names, pairs)]


def split_channels(sizes, pair_act, in_weights, out_weights, chain_lengths):
    rows, cols, width = pair_act.shape
    places, out_places = places_of(sizes, SIDES_ORDER), places_of(sizes, TRIANGLE_ORDER)
    n_col, n_row = len(places), len(places[0])
    group, half_group = n_col * n_row, n_col * n_row // 2
    per, half_per = width // group, width // half_group
    owner = {p: q for col, out_col in zip(places, out_places) for p, q in zip(col, out_col)}
    blocks = [owner[p] for p in range(group)]
    right_places = places_of(sizes, RIGHT_ORDER)
    half_places = places_of({**sizes, "row_a": 1}, HALF_ORDER + ("row_a",))
    half_owner = {p: q for col, half_col in zip(right_places, half_places) for p, q in zip(col, half_col * 2)}
    half_blocks = [half_owner[p] for p in range(group)]

    def shape_of(*dims, dtype=BF16):
        return jax.ShapeDtypeStruct(dims, dtype)

    block_shape = shape_of(rows, width, cols)
    part_shape = shape_of(4, half_per, rows, cols)
    scr = pltpu.VMEM((rows, width, cols), BF16)
    wt_scr = pltpu.VMEM((5 * width, width), BF16)
    flops_in = 2 * rows * cols * width * 5 * width
    flops_out = 2 * rows * cols * width * width
    flops_tri = 2 * group * rows * cols * width * rows * n_row

    def exchange(array, order):
        return lax.all_to_all(array, order, split_axis=0, concat_axis=0, tiled=True)

    right, *left, mask = call(
        functools.partial(first_kernel, half_blocks), "project",
        (shape_of(group, half_per, rows, cols),) + (part_shape,) * 4
        + (shape_of(rows, cols, dtype=F32),),
        [
            scr, scr, wt_scr, pltpu.SMEM(chain_lengths.shape, jnp.int32), pltpu.VMEM(pair_act.shape, BF16),
            pltpu.VMEM(in_weights.shape[1:], BF16), pltpu.VMEM((half_group, half_per, rows, cols), BF16),
            pltpu.SemaphoreType.DMA((3,)),
        ],
        [HBM, HBM, HBM], flops_in, chain_lengths, pair_act, in_weights, vmem=FIRST_VMEM_LIMIT,
    )
    right = exchange(right, RIGHT_ORDER)
    left = to_partners(left, ("row_b", "row_d"))
    left = call(regroup_kernel, "regroup", (part_shape,) * 4, [], [VM] * 4, 3000 * flops_out, *left, vmem=4 * 1024 * 1024)
    left = to_partners(left, ("row_c", "col"))
    gate, pair_t = call(
        gate_kernel, "gate", (block_shape, block_shape), [], [VM, VM], flops_out, pair_act, in_weights
    )
    tri = call(
        functools.partial(outgoing_kernel, right_places), "outgoing", shape_of(half_group, half_per, rows, cols),
        [], [VM] * 5 + [ANY], flops_tri, *left, right, gate,
    )
    tri = exchange(tri, HALF_ORDER).reshape(width, rows, cols)
    send, gate, pair_t = call(
        functools.partial(middle_kernel, blocks), "finish_project",
        (shape_of(group, 2, per, rows, cols), block_shape, block_shape),
        [scr, scr, wt_scr, scr], [VM] * 6, flops_in + flops_out,
        tri, gate, pair_t, mask, out_weights, in_weights,
    )
    recv = exchange(send, SIDES_ORDER)
    tri = call(
        functools.partial(incoming_kernel, places, out_places), "incoming", shape_of(group, per, rows, cols),
        [], [VM], flops_tri, recv,
    )
    tri = exchange(tri, TRIANGLE_ORDER).reshape(width, rows, cols)
    return call(
        last_kernel, "finish", shape_of(*pair_act.shape), [scr],
        [VM, VM, VM, VM], flops_out, tri, gate, pair_t, out_weights,
    )


def project(pair_act, weights, pair_mask):
    width = pair_act.shape[2]
    normed = layer_norm(pair_act.astype(F32), 2).astype(BF16)
    projected = jnp.einsum("rjd,de->erj", normed, weights[:, 0 : 4 * width], preferred_element_type=F32)
    left_vals = (jax.nn.sigmoid(projected[0:width]) * projected[width : 2 * width] * pair_mask).astype(BF16)
    right_vals = (
        jax.nn.sigmoid(projected[2 * width : 3 * width]) * projected[3 * width : 4 * width] * pair_mask
    ).astype(BF16)
    gate_vals = jax.nn.sigmoid(
        jnp.einsum("rjd,de->rje", normed, weights[:, 4 * width : 5 * width], preferred_element_type=F32)
    ).astype(BF16)
    return (left_vals, right_vals, gate_vals)


def to_channels(left_vals, right_vals):
    return (
        lax.all_to_all(left_vals, "row", split_axis=0, concat_axis=1, tiled=True),
        lax.all_to_all(right_vals, "row", split_axis=0, concat_axis=1, tiled=True),
    )


def finish(pair_act, triangle, gate_vals, weights_out):
    tri_normed = layer_norm(triangle.astype(F32), 0).astype(BF16)
    delta_vals = jnp.einsum("crj,cd->rjd", tri_normed, weights_out, preferred_element_type=F32)
    delta_vals = delta_vals * gate_vals.astype(F32)
    return (pair_act.astype(F32) + delta_vals).astype(BF16)


def split_rows(pair_act, in_weights, out_weights, chain_lengths):
    row_tile = pair_act.shape[0]
    col_tile = pair_act.shape[1]
    total_rows = row_tile * lax.axis_size("row")
    count_valid = total_rows - chain_lengths[chain_lengths.shape[0] - 1]
    row_first = lax.axis_index("row") * row_tile
    col_first = lax.axis_index("col") * col_tile
    row_valid = (row_first + jnp.arange(row_tile, dtype=jnp.int32) < count_valid).astype(F32)
    col_valid = (col_first + jnp.arange(col_tile, dtype=jnp.int32) < count_valid).astype(F32)
    pair_mask = row_valid[:, None] * col_valid[None, :]
    left_vals, right_vals, gate_vals = project(pair_act, in_weights[0], pair_mask)
    left_chan, right_chan = to_channels(left_vals, right_vals)
    left_rows = lax.all_to_all(left_chan, "col", split_axis=1, concat_axis=2, tiled=True)
    summed = jnp.einsum(
        "cik,cjk->cij",
        left_rows,
        lax.all_gather(right_chan, "col", axis=2, tiled=True),
        preferred_element_type=F32,
    )
    triangle = lax.all_to_all(
        lax.all_to_all(summed.astype(BF16), "col", split_axis=2, concat_axis=1, tiled=True),
        "row",
        split_axis=1,
        concat_axis=0,
        tiled=True,
    )
    first_pass = finish(pair_act, triangle, gate_vals, out_weights[0])
    left_vals, right_vals, gate_vals = project(first_pass, in_weights[1], pair_mask)
    left_chan, right_chan = to_channels(left_vals, right_vals)
    summed_in = jnp.einsum(
        "cki,ckj->cij",
        lax.all_gather(left_chan, "col", axis=2, tiled=True),
        right_chan,
        preferred_element_type=F32,
    ).astype(BF16)
    triangle_in = lax.all_to_all(summed_in, "row", split_axis=1, concat_axis=0, tiled=True)
    return finish(first_pass, triangle_in, gate_vals, out_weights[1])


def solution(mesh):
    n_parts, n_row, n_col = (mesh.shape[axis] for axis in ("parts", "row", "col"))

    def by_rows(*args):
        in_specs = (P(("parts", "row"), "col", None), P(), P(), P("parts"))
        return jax.shard_map(
            split_rows, mesh=mesh, in_specs=in_specs, out_specs=in_specs[0], check_vma=False
        )(*args)

    def by_channels(*args):
        shape = (n_parts, n_row // 8, 2, 2, 2, n_col)
        axes = ("parts",) + ROW_AXES + ("col",)
        fine = jax.sharding.Mesh(mesh.devices.reshape(shape), axes)
        in_specs = (P(axes[:-1], "col", None), P(), P(), P("parts"))
        return jax.shard_map(
            functools.partial(split_channels, dict(zip(axes, shape))),
            mesh=fine, in_specs=in_specs, out_specs=in_specs[0], check_vma=False,
        )(*args)

    def program(pair_act, in_weights, out_weights, chain_lengths):
        fits = n_row == 16 and n_col == 2 and pair_act.shape[2] % 32 == 0
        form = by_channels if fits else by_rows
        return form(pair_act, in_weights, out_weights, chain_lengths)

    return program
```

```python
import functools
import itertools

import jax
import jax.numpy as jnp
from jax import lax
from jax.experimental import pallas as pl
from jax.experimental.pallas import tpu as pltpu
from jax.sharding import PartitionSpec as P

epsilon = 1e-05
F32 = jnp.float32
BF16 = jnp.bfloat16
VMEM_LIMIT = 32 * 1024 * 1024
FIRST_VMEM_LIMIT = 56 * 1024 * 1024
ROW_AXES = ("row_a", "row_b", "row_c", "row_d")
RIGHT_ORDER = ("col", "row_d", "row_a", "row_c", "row_b")
SIDES_ORDER = ("col", "row_d", "row_c", "row_a", "row_b")
TRIANGLE_ORDER = ("col", "row_c", "row_b", "row_d", "row_a")
HALF_ORDER = ("row_c", "col", "row_d", "row_b")
FLIPS = ((0, 0), (0, 1), (1, 0), (1, 1))


def layer_norm(values, along_axis):
    mean_vals = jnp.mean(values, axis=along_axis, keepdims=True)
    centred = values - mean_vals
    variance = jnp.mean(centred * centred, axis=along_axis, keepdims=True)
    return centred * lax.rsqrt(variance + epsilon)


def sigmoid(values):
    return 0.5 * jnp.tanh(0.5 * values) + 0.5


def dot(lhs, rhs):
    return jnp.dot(lhs, rhs, preferred_element_type=F32)


def store_mask(ref, row_limit, col_limit):
    row = lax.broadcasted_iota(jnp.int32, ref.shape, 0)
    col = lax.broadcasted_iota(jnp.int32, ref.shape, 1)
    ref[...] = jnp.where(jnp.logical_and(row < row_limit, col < col_limit), 1.0, 0.0).astype(F32)


def load_mask(ref, first, group):
    return jnp.concatenate([ref[first + g : first + g + 1, :] for g in range(group)], axis=1)


def store_rows(ref, first, group, vals):
    cols = vals.shape[1] // group
    for g in range(group):
        ref[first + g] = vals[:, g * cols : (g + 1) * cols]


def load_rows(ref, first, group):
    return jnp.concatenate([ref[first + g] for g in range(group)], axis=1)


def project_side(normed, mask, weights_t, side):
    width = normed.shape[0]
    both = dot(weights_t[2 * side * width : (2 * side + 2) * width, :], normed)
    return (sigmoid(both[0:width]) * both[width : 2 * width] * mask).astype(BF16)


def project_rows(first, group, pair_vals, mask, weights_t, left_scr, right_scr, gate_ref):
    width = pair_vals.shape[0]
    normed = layer_norm(pair_vals, 0).astype(BF16)
    for side, scr in enumerate((left_scr, right_scr)):
        store_rows(scr, first, group, project_side(normed, mask, weights_t, side))
    gate = sigmoid(dot(weights_t[4 * width : 5 * width, :], normed))
    store_rows(gate_ref, first, group, gate.astype(BF16))


def send_channels(blocks, left_scr, right_scr, send_ref):
    per = send_ref.shape[2]
    for side, scr in enumerate((left_scr, right_scr)):
        swapped = jnp.swapaxes(scr[...], 0, 1)
        for place, block in enumerate(blocks):
            send_ref[place, side] = swapped[block * per : (block + 1) * per]


def half_place(col, row_c, row_b, row_d):
    at = {"col": col, "row_c": row_c, "row_b": row_b, "row_d": row_d}
    return functools.reduce(lambda place, axis: 2 * place + at[axis], HALF_ORDER, 0)


def flip(axis, by):
    at = lax.axis_index(axis)
    return 1 - at if by else at


def first_kernel(
    blocks, lengths_hbm, pair_hbm, weights_hbm, right_ref, own_ref, core_ref, z_ref, z_core_ref, mask_ref,
    left_scr, right_scr, wt_scr, lengths_scr, pair_scr, weights_scr, owner_scr, sems,
):
    rows, cols, width = pair_scr.shape
    group = rows
    fetches = [
        pltpu.make_async_copy(weights_hbm.at[0], weights_scr, sems.at[0]),
        pltpu.make_async_copy(pair_hbm, pair_scr, sems.at[1]),
        pltpu.make_async_copy(lengths_hbm, lengths_scr, sems.at[2]),
    ]
    for fetch in fetches:
        fetch.start()
    for fetch in fetches:
        fetch.wait()
    valid = rows * lax.axis_size(ROW_AXES) - lengths_scr[lengths_scr.shape[0] - 1]
    row_first = functools.reduce(lambda at, axis: at * lax.axis_size(axis) + lax.axis_index(axis), ROW_AXES, 0)
    store_mask(mask_ref, valid - row_first * rows, valid - lax.axis_index("col") * cols)
    wt_scr[...] = weights_scr[...].T
    for first in range(0, rows, group):
        pair = jnp.concatenate([pair_scr[first + g].T for g in range(group)], axis=1)
        normed = layer_norm(pair.astype(F32), 0).astype(BF16)
        mask = load_mask(mask_ref, first, group)
        for side, scr in enumerate((left_scr, right_scr)):
            store_rows(scr, first, group, project_side(normed, mask, wt_scr, side))
    per = right_ref.shape[1]
    swapped = jnp.swapaxes(right_scr[...], 0, 1)
    for place, block in enumerate(blocks):
        right_ref[place] = swapped[block * per : (block + 1) * per]
    owner_scr[...] = jnp.swapaxes(left_scr[...], 0, 1).reshape(owner_scr.shape)
    for part_ref, (by_z, by_core) in zip((own_ref, core_ref, z_ref, z_core_ref), FLIPS):
        for x_y in range(4):
            part_ref[x_y] = owner_scr[half_place(x_y // 2, x_y % 2, flip("row_b", by_z), flip("row_d", by_core))]


def gate_kernel(pair_ref, weights_ref, gate_ref, pair_t_ref):
    rows, cols, width = pair_ref.shape
    group = rows
    gate_t = weights_ref[0, :, 4 * width : 5 * width].T
    for first in range(0, rows, group):
        pair = jnp.concatenate([pair_ref[first + g].T for g in range(group)], axis=1)
        store_rows(pair_t_ref, first, group, pair)
        normed = layer_norm(pair.astype(F32), 0).astype(BF16)
        store_rows(gate_ref, first, group, sigmoid(dot(gate_t, normed)).astype(BF16))


def regroup_kernel(*refs):
    for part_ref, (by_y, by_x) in zip(refs[4:], FLIPS):
        at = flip("col", by_x) * 2 + flip("row_c", by_y)
        for sender in range(4):
            part_ref[sender] = refs[sender][at]


def finish_rows(first, group, tri_scr, wo_t, gate_ref, pair_t_ref):
    tri = load_rows(tri_scr, first, group).astype(F32)
    delta = dot(wo_t, layer_norm(tri, 0).astype(BF16))
    gate = load_rows(gate_ref, first, group).astype(F32)
    return (load_rows(pair_t_ref, first, group).astype(F32) + delta * gate).astype(BF16)


def middle_kernel(
    blocks, tri_ref, gate_in_ref, pair_t_in_ref, mask_ref, wo_ref, weights_ref,
    send_ref, gate_ref, pair_t_ref, left_scr, right_scr, wt_scr, tri_scr,
):
    width, rows, cols = tri_ref.shape
    group = rows
    wt_scr[...] = weights_ref[1].T
    wo_t = wo_ref[0].T
    tri_scr[...] = jnp.swapaxes(tri_ref[...], 0, 1)
    for first in range(0, rows, group):
        passed = finish_rows(first, group, tri_scr, wo_t, gate_in_ref, pair_t_in_ref)
        store_rows(pair_t_ref, first, group, passed)
        project_rows(
            first, group, passed.astype(F32), load_mask(mask_ref, first, group),
            wt_scr, left_scr, right_scr, gate_ref,
        )
    send_channels(blocks, left_scr, right_scr, send_ref)


def last_kernel(tri_ref, gate_ref, pair_t_ref, wo_ref, out_ref, tri_scr):
    width, rows, cols = tri_ref.shape
    group = rows
    wo_t = wo_ref[1].T
    tri_scr[...] = jnp.swapaxes(tri_ref[...], 0, 1)
    for first in range(0, rows, group):
        passed = finish_rows(first, group, tri_scr, wo_t, gate_ref, pair_t_ref)
        for g in range(group):
            out_ref[first + g] = passed[:, g * cols : (g + 1) * cols].T


def outgoing_kernel(places, *refs):
    left_refs, right_ref, out_ref = refs[:4], refs[4], refs[6]
    _, per, rows, cols = right_ref.shape
    first_col = lax.axis_index("col") == 0
    deltas = [(z_core, by_y) for z_core in range(4) for by_y in range(2)]
    for c in range(per):
        same, across = (
            jnp.concatenate([left_refs[2 * by_y + by_x][z_core, c] for z_core, by_y in deltas], axis=0)
            for by_x in (0, 1)
        )
        left = jnp.concatenate(
            [jnp.where(first_col, same, across), jnp.where(first_col, across, same)], axis=1
        )
        right = jnp.concatenate(
            [jnp.concatenate([right_ref[p, c] for p in column], axis=0) for column in places], axis=1
        )
        tri = lax.dot_general(
            left, right, (((1,), (1,)), ((), ())), preferred_element_type=F32
        ).astype(BF16)
        for block, (z_core, by_y) in enumerate(deltas):
            by_z, by_core = FLIPS[z_core]
            at = flip("row_c", by_y), flip("row_b", by_z), flip("row_d", by_core)
            for x in range(len(places)):
                out_ref[half_place(x, *at), c] = tri[block * rows : (block + 1) * rows, x * cols : (x + 1) * cols]


def incoming_kernel(places, out_places, recv_ref, out_ref):
    _, _, per, rows, cols = recv_ref.shape
    for c in range(per):
        left, right = (
            jnp.concatenate(
                [jnp.concatenate([recv_ref[p, side, c] for p in column], axis=0) for column in places], axis=1
            )
            for side in (0, 1)
        )
        tri = lax.dot_general(
            left, right, (((0,), (0,)), ((), ())), preferred_element_type=F32
        ).astype(BF16)
        for x, column in enumerate(out_places):
            for r, p in enumerate(column):
                out_ref[p, c] = tri[r * rows : (r + 1) * rows, x * cols : (x + 1) * cols]


def call(kernel, name, out_shape, scratch, in_specs, flops, *args, vmem=VMEM_LIMIT):
    return pl.pallas_call(
        kernel,
        name=name,
        out_shape=out_shape,
        in_specs=in_specs,
        out_specs=jax.tree.map(lambda _: pl.BlockSpec(memory_space=pltpu.VMEM), out_shape),
        scratch_shapes=scratch,
        compiler_params=pltpu.CompilerParams(vmem_limit_bytes=vmem),
        cost_estimate=pl.CostEstimate(flops=flops, bytes_accessed=2 << 20, transcendentals=0),
    )(*args)


VM = pl.BlockSpec(memory_space=pltpu.VMEM)
HBM = pl.BlockSpec(memory_space=pltpu.HBM)
ANY = pl.BlockSpec(memory_space=pl.ANY)


def places_of(sizes, order):
    places = {}
    for place, index in enumerate(itertools.product(*(range(sizes[axis]) for axis in order))):
        at = dict(zip(order, index))
        row = 0
        for axis in ROW_AXES:
            row = row * sizes[axis] + at[axis]
        places[at["col"], row] = place
    n_col, n_row = sizes["col"], len(places) // sizes["col"]
    return [[places[x, r] for r in range(n_row)] for x in range(n_col)]


def to_partners(parts, axes):
    pairs = [[(0, 1), (1, 0)], [(0, 1), (1, 0)], [(0, 3), (1, 2), (2, 1), (3, 0)]]
    names = (axes[1], axes[0], axes)
    return [parts[0]] + [lax.ppermute(p, name, pair) for p, name, pair in zip(parts[1:], names, pairs)]


def split_channels(sizes, pair_act, in_weights, out_weights, chain_lengths):
    rows, cols, width = pair_act.shape
    places, out_places = places_of(sizes, SIDES_ORDER), places_of(sizes, TRIANGLE_ORDER)
    n_col, n_row = len(places), len(places[0])
    group, half_group = n_col * n_row, n_col * n_row // 2
    per, half_per = width // group, width // half_group
    owner = {p: q for col, out_col in zip(places, out_places) for p, q in zip(col, out_col)}
    blocks = [owner[p] for p in range(group)]
    right_places = places_of(sizes, RIGHT_ORDER)
    half_places = places_of({**sizes, "row_a": 1}, HALF_ORDER + ("row_a",))
    half_owner = {p: q for col, half_col in zip(right_places, half_places) for p, q in zip(col, half_col * 2)}
    half_blocks = [half_owner[p] for p in range(group)]

    def shape_of(*dims, dtype=BF16):
        return jax.ShapeDtypeStruct(dims, dtype)

    block_shape = shape_of(rows, width, cols)
    part_shape = shape_of(4, half_per, rows, cols)
    scr = pltpu.VMEM((rows, width, cols), BF16)
    wt_scr = pltpu.VMEM((5 * width, width), BF16)
    flops_in = 2 * rows * cols * width * 5 * width
    flops_out = 2 * rows * cols * width * width
    flops_tri = 2 * group * rows * cols * width * rows * n_row

    def exchange(array, order):
        return lax.all_to_all(array, order, split_axis=0, concat_axis=0, tiled=True)

    right, *left, mask = call(
        functools.partial(first_kernel, half_blocks), "project",
        (shape_of(group, half_per, rows, cols),) + (part_shape,) * 4
        + (shape_of(rows, cols, dtype=F32),),
        [
            scr, scr, wt_scr, pltpu.SMEM(chain_lengths.shape, jnp.int32), pltpu.VMEM(pair_act.shape, BF16),
            pltpu.VMEM(in_weights.shape[1:], BF16), pltpu.VMEM((half_group, half_per, rows, cols), BF16),
            pltpu.SemaphoreType.DMA((3,)),
        ],
        [HBM, HBM, HBM], flops_in, chain_lengths, pair_act, in_weights, vmem=FIRST_VMEM_LIMIT,
    )
    right = exchange(right, RIGHT_ORDER)
    left = to_partners(left, ("row_b", "row_d"))
    left = call(regroup_kernel, "regroup", (part_shape,) * 4, [], [VM] * 4, 3000 * flops_out, *left, vmem=4 * 1024 * 1024)
    left = to_partners(left, ("row_c", "col"))
    gate, pair_t = call(
        gate_kernel, "gate", (block_shape, block_shape), [], [VM, VM], flops_out, pair_act, in_weights
    )
    tri = call(
        functools.partial(outgoing_kernel, right_places), "outgoing", shape_of(half_group, half_per, rows, cols),
        [], [VM] * 5 + [ANY], flops_tri, *left, right, gate,
    )
    tri = exchange(tri, HALF_ORDER).reshape(width, rows, cols)
    send, gate, pair_t = call(
        functools.partial(middle_kernel, blocks), "finish_project",
        (shape_of(group, 2, per, rows, cols), block_shape, block_shape),
        [scr, scr, wt_scr, scr], [VM] * 6, flops_in + flops_out,
        tri, gate, pair_t, mask, out_weights, in_weights,
    )
    recv = exchange(send, SIDES_ORDER)
    tri = call(
        functools.partial(incoming_kernel, places, out_places), "incoming", shape_of(group, per, rows, cols),
        [], [VM], flops_tri, recv,
    )
    tri = exchange(tri, TRIANGLE_ORDER).reshape(width, rows, cols)
    return call(
        last_kernel, "finish", shape_of(*pair_act.shape), [scr],
        [VM, VM, VM, VM], flops_out, tri, gate, pair_t, out_weights,
    )


def project(pair_act, weights, pair_mask):
    width = pair_act.shape[2]
    normed = layer_norm(pair_act.astype(F32), 2).astype(BF16)
    projected = jnp.einsum("rjd,de->erj", normed, weights[:, 0 : 4 * width], preferred_element_type=F32)
    left_vals = (jax.nn.sigmoid(projected[0:width]) * projected[width : 2 * width] * pair_mask).astype(BF16)
    right_vals = (
        jax.nn.sigmoid(projected[2 * width : 3 * width]) * projected[3 * width : 4 * width] * pair_mask
    ).astype(BF16)
    gate_vals = jax.nn.sigmoid(
        jnp.einsum("rjd,de->rje", normed, weights[:, 4 * width : 5 * width], preferred_element_type=F32)
    ).astype(BF16)
    return (left_vals, right_vals, gate_vals)


def to_channels(left_vals, right_vals):
    return (
        lax.all_to_all(left_vals, "row", split_axis=0, concat_axis=1, tiled=True),
        lax.all_to_all(right_vals, "row", split_axis=0, concat_axis=1, tiled=True),
    )


def finish(pair_act, triangle, gate_vals, weights_out):
    tri_normed = layer_norm(triangle.astype(F32), 0).astype(BF16)
    delta_vals = jnp.einsum("crj,cd->rjd", tri_normed, weights_out, preferred_element_type=F32)
    delta_vals = delta_vals * gate_vals.astype(F32)
    return (pair_act.astype(F32) + delta_vals).astype(BF16)


def split_rows(pair_act, in_weights, out_weights, chain_lengths):
    row_tile = pair_act.shape[0]
    col_tile = pair_act.shape[1]
    total_rows = row_tile * lax.axis_size("row")
    count_valid = total_rows - chain_lengths[chain_lengths.shape[0] - 1]
    row_first = lax.axis_index("row") * row_tile
    col_first = lax.axis_index("col") * col_tile
    row_valid = (row_first + jnp.arange(row_tile, dtype=jnp.int32) < count_valid).astype(F32)
    col_valid = (col_first + jnp.arange(col_tile, dtype=jnp.int32) < count_valid).astype(F32)
    pair_mask = row_valid[:, None] * col_valid[None, :]
    left_vals, right_vals, gate_vals = project(pair_act, in_weights[0], pair_mask)
    left_chan, right_chan = to_channels(left_vals, right_vals)
    left_rows = lax.all_to_all(left_chan, "col", split_axis=1, concat_axis=2, tiled=True)
    summed = jnp.einsum(
        "cik,cjk->cij",
        left_rows,
        lax.all_gather(right_chan, "col", axis=2, tiled=True),
        preferred_element_type=F32,
    )
    triangle = lax.all_to_all(
        lax.all_to_all(summed.astype(BF16), "col", split_axis=2, concat_axis=1, tiled=True),
        "row",
        split_axis=1,
        concat_axis=0,
        tiled=True,
    )
    first_pass = finish(pair_act, triangle, gate_vals, out_weights[0])
    left_vals, right_vals, gate_vals = project(first_pass, in_weights[1], pair_mask)
    left_chan, right_chan = to_channels(left_vals, right_vals)
    summed_in = jnp.einsum(
        "cki,ckj->cij",
        lax.all_gather(left_chan, "col", axis=2, tiled=True),
        right_chan,
        preferred_element_type=F32,
    ).astype(BF16)
    triangle_in = lax.all_to_all(summed_in, "row", split_axis=1, concat_axis=0, tiled=True)
    return finish(first_pass, triangle_in, gate_vals, out_weights[1])


def solution(mesh):
    n_parts, n_row, n_col = (mesh.shape[axis] for axis in ("parts", "row", "col"))

    def by_rows(*args):
        in_specs = (P(("parts", "row"), "col", None), P(), P(), P("parts"))
        return jax.shard_map(
            split_rows, mesh=mesh, in_specs=in_specs, out_specs=in_specs[0], check_vma=False
        )(*args)

    def by_channels(*args):
        shape = (n_parts, n_row // 8, 2, 2, 2, n_col)
        axes = ("parts",) + ROW_AXES + ("col",)
        fine = jax.sharding.Mesh(mesh.devices.reshape(shape), axes)
        in_specs = (P(axes[:-1], "col", None), P(), P(), P("parts"))
        return jax.shard_map(
            functools.partial(split_channels, dict(zip(axes, shape))),
            mesh=fine, in_specs=in_specs, out_specs=in_specs[0], check_vma=False,
        )(*args)

    def program(pair_act, in_weights, out_weights, chain_lengths):
        fits = n_row == 16 and n_col == 2 and pair_act.shape[2] % 32 == 0
        form = by_channels if fits else by_rows
        return form(pair_act, in_weights, out_weights, chain_lengths)

    return program
```

```python
import functools
import itertools

import jax
import jax.numpy as jnp
from jax import lax
from jax.experimental import pallas as pl
from jax.experimental.pallas import tpu as pltpu
from jax.sharding import PartitionSpec as P

epsilon = 1e-05
F32 = jnp.float32
BF16 = jnp.bfloat16
VMEM_LIMIT = 32 * 1024 * 1024
FIRST_VMEM_LIMIT = 54 * 1024 * 1024
ROW_AXES = ("row_a", "row_b", "row_c", "row_d")
RIGHT_ORDER = ("col", "row_d", "row_a", "row_c", "row_b")
SIDES_ORDER = ("col", "row_d", "row_c", "row_a", "row_b")
TRIANGLE_ORDER = ("col", "row_c", "row_b", "row_d", "row_a")
HALF_ORDER = ("row_c", "col", "row_d", "row_b")
FLIPS = ((0, 0), (0, 1), (1, 0), (1, 1))


def layer_norm(values, along_axis):
    mean_vals = jnp.mean(values, axis=along_axis, keepdims=True)
    centred = values - mean_vals
    variance = jnp.mean(centred * centred, axis=along_axis, keepdims=True)
    return centred * lax.rsqrt(variance + epsilon)


def sigmoid(values):
    return 0.5 * jnp.tanh(0.5 * values) + 0.5


def dot(lhs, rhs):
    return jnp.dot(lhs, rhs, preferred_element_type=F32)


def store_mask(ref, row_limit, col_limit):
    row = lax.broadcasted_iota(jnp.int32, ref.shape, 0)
    col = lax.broadcasted_iota(jnp.int32, ref.shape, 1)
    ref[...] = jnp.where(jnp.logical_and(row < row_limit, col < col_limit), 1.0, 0.0).astype(F32)


def load_mask(ref, first, group):
    return jnp.concatenate([ref[first + g : first + g + 1, :] for g in range(group)], axis=1)


def store_rows(ref, first, group, vals):
    cols = vals.shape[1] // group
    for g in range(group):
        ref[first + g] = vals[:, g * cols : (g + 1) * cols]


def load_rows(ref, first, group):
    return jnp.concatenate([ref[first + g] for g in range(group)], axis=1)


def project_side(normed, mask, weights_t, side):
    width = normed.shape[0]
    both = dot(weights_t[2 * side * width : (2 * side + 2) * width, :], normed)
    return (sigmoid(both[0:width]) * both[width : 2 * width] * mask).astype(BF16)


def project_rows(first, group, pair_vals, mask, weights_t, left_scr, right_scr, gate_ref):
    width = pair_vals.shape[0]
    normed = layer_norm(pair_vals, 0).astype(BF16)
    for side, scr in enumerate((left_scr, right_scr)):
        store_rows(scr, first, group, project_side(normed, mask, weights_t, side))
    gate = sigmoid(dot(weights_t[4 * width : 5 * width, :], normed))
    store_rows(gate_ref, first, group, gate.astype(BF16))


def send_channels(blocks, left_scr, right_scr, send_ref):
    per = send_ref.shape[2]
    for side, scr in enumerate((left_scr, right_scr)):
        swapped = jnp.swapaxes(scr[...], 0, 1)
        for place, block in enumerate(blocks):
            send_ref[place, side] = swapped[block * per : (block + 1) * per]


def half_place(col, row_c, row_b, row_d):
    at = {"col": col, "row_c": row_c, "row_b": row_b, "row_d": row_d}
    return functools.reduce(lambda place, axis: 2 * place + at[axis], HALF_ORDER, 0)


def flip(axis, by):
    at = lax.axis_index(axis)
    return 1 - at if by else at


def first_kernel(
    blocks, lengths_hbm, pair_hbm, weights_hbm, right_ref, own_ref, core_ref, z_ref, z_core_ref, mask_ref,
    left_scr, right_scr, wt_scr, lengths_scr, pair_scr, weights_scr, owner_scr, sems,
):
    rows, cols, width = pair_scr.shape
    group = rows
    fetches = [
        pltpu.make_async_copy(weights_hbm.at[0], weights_scr, sems.at[0]),
        pltpu.make_async_copy(pair_hbm, pair_scr, sems.at[1]),
        pltpu.make_async_copy(lengths_hbm, lengths_scr, sems.at[2]),
    ]
    for fetch in fetches:
        fetch.start()
    for fetch in fetches:
        fetch.wait()
    valid = rows * lax.axis_size(ROW_AXES) - lengths_scr[lengths_scr.shape[0] - 1]
    row_first = functools.reduce(lambda at, axis: at * lax.axis_size(axis) + lax.axis_index(axis), ROW_AXES, 0)
    store_mask(mask_ref, valid - row_first * rows, valid - lax.axis_index("col") * cols)
    wt_scr[...] = weights_scr[...].T
    for first in range(0, rows, group):
        pair = jnp.concatenate([pair_scr[first + g].T for g in range(group)], axis=1)
        normed = layer_norm(pair.astype(F32), 0).astype(BF16)
        mask = load_mask(mask_ref, first, group)
        for side, scr in enumerate((left_scr, right_scr)):
            store_rows(scr, first, group, project_side(normed, mask, wt_scr, side))
    per = right_ref.shape[1]
    swapped = jnp.swapaxes(right_scr[...], 0, 1)
    for place, block in enumerate(blocks):
        right_ref[place] = swapped[block * per : (block + 1) * per]
    owner_scr[...] = jnp.swapaxes(left_scr[...], 0, 1).reshape(owner_scr.shape)
    for part_ref, (by_z, by_core) in zip((own_ref, core_ref, z_ref, z_core_ref), FLIPS):
        for x_y in range(4):
            part_ref[x_y] = owner_scr[half_place(x_y // 2, x_y % 2, flip("row_b", by_z), flip("row_d", by_core))]


def gate_kernel(pair_ref, weights_ref, wo_ref, gate_ref, pair_t_ref, wt_ref, wo_t_ref, last_wo_t_ref):
    rows, cols, width = pair_ref.shape
    group = rows
    gate_t = weights_ref[0, :, 4 * width : 5 * width].T
    wt_ref[...] = weights_ref[1].T
    wo_t_ref[...] = wo_ref[0].T
    last_wo_t_ref[...] = wo_ref[1].T
    for first in range(0, rows, group):
        pair = jnp.concatenate([pair_ref[first + g].T for g in range(group)], axis=1)
        store_rows(pair_t_ref, first, group, pair)
        normed = layer_norm(pair.astype(F32), 0).astype(BF16)
        store_rows(gate_ref, first, group, sigmoid(dot(gate_t, normed)).astype(BF16))


def regroup_kernel(*refs):
    for part_ref, (by_y, by_x) in zip(refs[4:], FLIPS):
        at = flip("col", by_x) * 2 + flip("row_c", by_y)
        for sender in range(4):
            part_ref[sender] = refs[sender][at]


def finish_rows(first, group, tri_scr, wo_t, gate_ref, pair_t_ref):
    tri = load_rows(tri_scr, first, group).astype(F32)
    delta = dot(wo_t, layer_norm(tri, 0).astype(BF16))
    gate = load_rows(gate_ref, first, group).astype(F32)
    return (load_rows(pair_t_ref, first, group).astype(F32) + delta * gate).astype(BF16)


def middle_kernel(
    blocks, tri_ref, gate_in_ref, pair_t_in_ref, mask_ref, wo_t_ref, wt_ref,
    send_ref, gate_ref, pair_t_ref, left_scr, right_scr, tri_scr,
):
    width, rows, cols = tri_ref.shape
    group = rows
    tri_scr[...] = jnp.swapaxes(tri_ref[...], 0, 1)
    for first in range(0, rows, group):
        passed = finish_rows(first, group, tri_scr, wo_t_ref[...], gate_in_ref, pair_t_in_ref)
        store_rows(pair_t_ref, first, group, passed)
        project_rows(
            first, group, passed.astype(F32), load_mask(mask_ref, first, group),
            wt_ref, left_scr, right_scr, gate_ref,
        )
    send_channels(blocks, left_scr, right_scr, send_ref)


def last_kernel(tri_ref, gate_ref, pair_t_ref, wo_t_ref, out_hbm, tri_scr, out_scr, sems):
    width, rows, cols = tri_ref.shape
    group = rows // sems.shape[0]
    tri_scr[...] = jnp.swapaxes(tri_ref[...], 0, 1)
    stores = []
    for first in range(0, rows, group):
        passed = finish_rows(first, group, tri_scr, wo_t_ref[...], gate_ref, pair_t_ref)
        for g in range(group):
            out_scr[first + g] = passed[:, g * cols : (g + 1) * cols].T
        at = pl.ds(first, group)
        stores.append(pltpu.make_async_copy(out_scr.at[at], out_hbm.at[at], sems.at[first // group]))
        stores[-1].start()
    for store in stores:
        store.wait()


def outgoing_kernel(places, *refs):
    left_refs, right_ref, out_ref = refs[:4], refs[4], refs[6]
    _, per, rows, cols = right_ref.shape
    first_col = lax.axis_index("col") == 0
    deltas = [(z_core, by_y) for z_core in range(4) for by_y in range(2)]
    for c in range(per):
        same, across = (
            jnp.concatenate([left_refs[2 * by_y + by_x][z_core, c] for z_core, by_y in deltas], axis=0)
            for by_x in (0, 1)
        )
        left = jnp.concatenate(
            [jnp.where(first_col, same, across), jnp.where(first_col, across, same)], axis=1
        )
        right = jnp.concatenate(
            [jnp.concatenate([right_ref[p, c] for p in column], axis=0) for column in places], axis=1
        )
        tri = lax.dot_general(
            left, right, (((1,), (1,)), ((), ())), preferred_element_type=F32
        ).astype(BF16)
        for block, (z_core, by_y) in enumerate(deltas):
            by_z, by_core = FLIPS[z_core]
            at = flip("row_c", by_y), flip("row_b", by_z), flip("row_d", by_core)
            for x in range(len(places)):
                out_ref[half_place(x, *at), c] = tri[block * rows : (block + 1) * rows, x * cols : (x + 1) * cols]


def incoming_kernel(places, out_places, recv_ref, out_ref):
    _, _, per, rows, cols = recv_ref.shape
    for c in range(per):
        left, right = (
            jnp.concatenate(
                [jnp.concatenate([recv_ref[p, side, c] for p in column], axis=0) for column in places], axis=1
            )
            for side in (0, 1)
        )
        tri = lax.dot_general(
            left, right, (((0,), (0,)), ((), ())), preferred_element_type=F32
        ).astype(BF16)
        for x, column in enumerate(out_places):
            for r, p in enumerate(column):
                out_ref[p, c] = tri[r * rows : (r + 1) * rows, x * cols : (x + 1) * cols]


def call(kernel, name, out_shape, scratch, in_specs, flops, *args, vmem=VMEM_LIMIT, out_specs=None):
    return pl.pallas_call(
        kernel,
        name=name,
        out_shape=out_shape,
        in_specs=in_specs,
        out_specs=out_specs or jax.tree.map(lambda _: VM, out_shape),
        scratch_shapes=scratch,
        compiler_params=pltpu.CompilerParams(vmem_limit_bytes=vmem),
        cost_estimate=pl.CostEstimate(flops=flops, bytes_accessed=2 << 20, transcendentals=0),
    )(*args)


VM = pl.BlockSpec(memory_space=pltpu.VMEM)
HBM = pl.BlockSpec(memory_space=pltpu.HBM)
ANY = pl.BlockSpec(memory_space=pl.ANY)


def places_of(sizes, order):
    places = {}
    for place, index in enumerate(itertools.product(*(range(sizes[axis]) for axis in order))):
        at = dict(zip(order, index))
        row = 0
        for axis in ROW_AXES:
            row = row * sizes[axis] + at[axis]
        places[at["col"], row] = place
    n_col, n_row = sizes["col"], len(places) // sizes["col"]
    return [[places[x, r] for r in range(n_row)] for x in range(n_col)]


def to_partners(parts, axes):
    pairs = [[(0, 1), (1, 0)], [(0, 1), (1, 0)], [(0, 3), (1, 2), (2, 1), (3, 0)]]
    names = (axes[1], axes[0], axes)
    return [parts[0]] + [lax.ppermute(p, name, pair) for p, name, pair in zip(parts[1:], names, pairs)]


def split_channels(sizes, pair_act, in_weights, out_weights, chain_lengths):
    rows, cols, width = pair_act.shape
    places, out_places = places_of(sizes, SIDES_ORDER), places_of(sizes, TRIANGLE_ORDER)
    n_col, n_row = len(places), len(places[0])
    group, half_group = n_col * n_row, n_col * n_row // 2
    per, half_per = width // group, width // half_group
    owner = {p: q for col, out_col in zip(places, out_places) for p, q in zip(col, out_col)}
    blocks = [owner[p] for p in range(group)]
    right_places = places_of(sizes, RIGHT_ORDER)
    half_places = places_of({**sizes, "row_a": 1}, HALF_ORDER + ("row_a",))
    half_owner = {p: q for col, half_col in zip(right_places, half_places) for p, q in zip(col, half_col * 2)}
    half_blocks = [half_owner[p] for p in range(group)]

    def shape_of(*dims, dtype=BF16):
        return jax.ShapeDtypeStruct(dims, dtype)

    block_shape = shape_of(rows, width, cols)
    part_shape = shape_of(4, half_per, rows, cols)
    scr = pltpu.VMEM((rows, width, cols), BF16)
    wt_scr = pltpu.VMEM((5 * width, width), BF16)
    flops_in = 2 * rows * cols * width * 5 * width
    flops_out = 2 * rows * cols * width * width
    flops_tri = 2 * group * rows * cols * width * rows * n_row

    def exchange(array, order):
        return lax.all_to_all(array, order, split_axis=0, concat_axis=0, tiled=True)

    right, *left, mask = call(
        functools.partial(first_kernel, half_blocks), "project",
        (shape_of(group, half_per, rows, cols),) + (pltpu.VMEM(part_shape.shape, BF16),) * 4
        + (pltpu.VMEM((rows, cols), F32),),
        [
            scr, scr, wt_scr, pltpu.SMEM(chain_lengths.shape, jnp.int32), pltpu.VMEM(pair_act.shape, BF16),
            pltpu.VMEM(in_weights.shape[1:], BF16), pltpu.VMEM((half_group, half_per, rows, cols), BF16),
            pltpu.SemaphoreType.DMA((3,)),
        ],
        [HBM, HBM, HBM], flops_in, chain_lengths, pair_act, in_weights, vmem=FIRST_VMEM_LIMIT,
    )
    right = exchange(right, RIGHT_ORDER)
    left = to_partners(left, ("row_b", "row_d"))
    left = call(regroup_kernel, "regroup", (part_shape,) * 4, [], [VM] * 4, 3000 * flops_out, *left, vmem=4 * 1024 * 1024)
    left = to_partners(left, ("row_c", "col"))
    wo_shape = shape_of(width, width)
    gate, pair_t, wt, wo_t, last_wo_t = call(
        gate_kernel, "gate", (block_shape, block_shape, shape_of(5 * width, width), wo_shape, wo_shape), [],
        [VM] * 3, flops_out, pair_act, in_weights, out_weights,
    )
    tri = call(
        functools.partial(outgoing_kernel, right_places), "outgoing", shape_of(half_group, half_per, rows, cols),
        [], [VM] * 5 + [ANY], flops_tri, *left, right, gate,
    )
    tri = exchange(tri, HALF_ORDER).reshape(width, rows, cols)
    send, gate, pair_t = call(
        functools.partial(middle_kernel, blocks), "finish_project",
        (shape_of(group, 2, per, rows, cols), block_shape, block_shape),
        [scr, scr, scr], [VM] * 6, flops_in + flops_out, tri, gate, pair_t, mask, wo_t, wt,
    )
    recv = exchange(send, SIDES_ORDER)
    tri = call(
        functools.partial(incoming_kernel, places, out_places), "incoming", shape_of(group, per, rows, cols),
        [], [VM], flops_tri, recv,
    )
    tri = exchange(tri, TRIANGLE_ORDER).reshape(width, rows, cols)
    return call(
        last_kernel, "finish", shape_of(*pair_act.shape),
        [scr, pltpu.VMEM(pair_act.shape, BF16), pltpu.SemaphoreType.DMA((4,))],
        [VM, VM, VM, VM], flops_out, tri, gate, pair_t, last_wo_t, out_specs=HBM,
    )


def project(pair_act, weights, pair_mask):
    width = pair_act.shape[2]
    normed = layer_norm(pair_act.astype(F32), 2).astype(BF16)
    projected = jnp.einsum("rjd,de->erj", normed, weights[:, 0 : 4 * width], preferred_element_type=F32)
    left_vals = (jax.nn.sigmoid(projected[0:width]) * projected[width : 2 * width] * pair_mask).astype(BF16)
    right_vals = (
        jax.nn.sigmoid(projected[2 * width : 3 * width]) * projected[3 * width : 4 * width] * pair_mask
    ).astype(BF16)
    gate_vals = jax.nn.sigmoid(
        jnp.einsum("rjd,de->rje", normed, weights[:, 4 * width : 5 * width], preferred_element_type=F32)
    ).astype(BF16)
    return (left_vals, right_vals, gate_vals)


def to_channels(left_vals, right_vals):
    return (
        lax.all_to_all(left_vals, "row", split_axis=0, concat_axis=1, tiled=True),
        lax.all_to_all(right_vals, "row", split_axis=0, concat_axis=1, tiled=True),
    )


def finish(pair_act, triangle, gate_vals, weights_out):
    tri_normed = layer_norm(triangle.astype(F32), 0).astype(BF16)
    delta_vals = jnp.einsum("crj,cd->rjd", tri_normed, weights_out, preferred_element_type=F32)
    delta_vals = delta_vals * gate_vals.astype(F32)
    return (pair_act.astype(F32) + delta_vals).astype(BF16)


def split_rows(pair_act, in_weights, out_weights, chain_lengths):
    row_tile = pair_act.shape[0]
    col_tile = pair_act.shape[1]
    total_rows = row_tile * lax.axis_size("row")
    count_valid = total_rows - chain_lengths[chain_lengths.shape[0] - 1]
    row_first = lax.axis_index("row") * row_tile
    col_first = lax.axis_index("col") * col_tile
    row_valid = (row_first + jnp.arange(row_tile, dtype=jnp.int32) < count_valid).astype(F32)
    col_valid = (col_first + jnp.arange(col_tile, dtype=jnp.int32) < count_valid).astype(F32)
    pair_mask = row_valid[:, None] * col_valid[None, :]
    left_vals, right_vals, gate_vals = project(pair_act, in_weights[0], pair_mask)
    left_chan, right_chan = to_channels(left_vals, right_vals)
    left_rows = lax.all_to_all(left_chan, "col", split_axis=1, concat_axis=2, tiled=True)
    summed = jnp.einsum(
        "cik,cjk->cij",
        left_rows,
        lax.all_gather(right_chan, "col", axis=2, tiled=True),
        preferred_element_type=F32,
    )
    triangle = lax.all_to_all(
        lax.all_to_all(summed.astype(BF16), "col", split_axis=2, concat_axis=1, tiled=True),
        "row",
        split_axis=1,
        concat_axis=0,
        tiled=True,
    )
    first_pass = finish(pair_act, triangle, gate_vals, out_weights[0])
    left_vals, right_vals, gate_vals = project(first_pass, in_weights[1], pair_mask)
    left_chan, right_chan = to_channels(left_vals, right_vals)
    summed_in = jnp.einsum(
        "cki,ckj->cij",
        lax.all_gather(left_chan, "col", axis=2, tiled=True),
        right_chan,
        preferred_element_type=F32,
    ).astype(BF16)
    triangle_in = lax.all_to_all(summed_in, "row", split_axis=1, concat_axis=0, tiled=True)
    return finish(first_pass, triangle_in, gate_vals, out_weights[1])


def solution(mesh):
    n_parts, n_row, n_col = (mesh.shape[axis] for axis in ("parts", "row", "col"))

    def by_rows(*args):
        in_specs = (P(("parts", "row"), "col", None), P(), P(), P("parts"))
        return jax.shard_map(
            split_rows, mesh=mesh, in_specs=in_specs, out_specs=in_specs[0], check_vma=False
        )(*args)

    def by_channels(*args):
        shape = (n_parts, n_row // 8, 2, 2, 2, n_col)
        axes = ("parts",) + ROW_AXES + ("col",)
        fine = jax.sharding.Mesh(mesh.devices.reshape(shape), axes)
        in_specs = (P(axes[:-1], "col", None), P(), P(), P("parts"))
        return jax.shard_map(
            functools.partial(split_channels, dict(zip(axes, shape))),
            mesh=fine, in_specs=in_specs, out_specs=in_specs[0], check_vma=False,
        )(*args)

    def program(pair_act, in_weights, out_weights, chain_lengths):
        fits = n_row == 16 and n_col == 2 and pair_act.shape[2] % 32 == 0
        form = by_channels if fits else by_rows
        return form(pair_act, in_weights, out_weights, chain_lengths)

    return program
```
